32 devices in a mesh: blk: 16 (over z, y, core), split: 2 (over x).
Axes of the slice: x: 2, y: 2, z: 4, core: 2. Of those that a mesh axis runs over, the one named last changes fastest.
Arguments:
- user_factors: float32 [8192, 512], P(('blk', 'split')), may hold values from -2 to 2
- item_factors: float32 [2048, 512], P('blk'), may hold values from -2 to 2
- obs_items: int32 [8192, 4, 8], P(('blk', 'split')), may hold values from 0 to 127
- obs_conf: int32 [8192, 4, 8], P(('blk', 'split')), may hold values from 1 to 3
Outputs:
- users_out: float32 [8192, 512], P(('blk', 'split'))
- items_out: float32 [2048, 512], P(('blk', 'split'))
The draws below stay inside these ranges and needn't reach their ends.
All inputs are finite; a program needn't handle non-finite values.
Results may differ from the reference program's by a relative error of at most 0.0003.
Values sent between devices are 32-bit elements; how exact they have to be, the bound alone decides.
A program may use at most 64 MiB of HBM per device.

```python
import jax
import jax.numpy as jnp
from jax import lax

R = 512
U_DEV = 256
I_SLAB = 128
OBS = 8
SUBS = 4
USERS = 8192
ITEMS = 2048
N_BLK = 16
N_SPLIT = 2


def touch_ends(drawn, rng, least, largest):
    index_at = [jax.random.randint(jax.random.fold_in(rng, axis), (), 0, length) for axis, length in enumerate(drawn.shape)]
    longest = drawn.shape.index(max(drawn.shape))
    neighbour = index_at[:longest] + [(index_at[longest] + 1) % drawn.shape[longest]] + index_at[longest + 1:]
    return drawn.at[tuple(index_at)].set(least).at[tuple(neighbour)].set(largest)


def steps_of(stream_key, extent, split, least, largest):
    loudness, own = 1.0, jax.random.fold_in(stream_key, 6)
    for axis_at, blocks in split:
        draws = jnp.exp(jax.random.uniform(jax.random.fold_in(own, axis_at), (blocks,), jnp.float32, least / len(split), largest / len(split)))
        loudness = loudness * jnp.repeat(draws, extent[axis_at] // blocks).reshape([-1 if axis == axis_at else 1 for axis in range(len(extent))])
    return loudness


def noise(stream_key, extent, width, bound, split=(), kind=jnp.bfloat16):
    values = width * jax.random.normal(stream_key, extent, jnp.float32)
    if split:
        values = values * steps_of(stream_key, extent, split, -0.22, 0.18)
    return jnp.clip(values, -bound, bound).astype(kind)


def setup_inputs(seed: int = 0) -> dict:
    streams_of = jax.random.split(jax.random.key(seed), 5)
    user_factors = noise(streams_of[0], (USERS, R), 0.25, 2.0, ((0, 32),), jnp.float32)
    item_factors = noise(streams_of[1], (ITEMS, R), 0.25, 2.0, ((0, 16),), jnp.float32)
    obs_items = touch_ends(jax.random.randint(streams_of[2], (USERS, SUBS, OBS), 0, I_SLAB), jax.random.fold_in(streams_of[2], 1), 0, I_SLAB - 1).astype(jnp.int32)
    obs_conf = touch_ends(jax.random.randint(streams_of[3], (USERS, SUBS, OBS), 1, 4), jax.random.fold_in(streams_of[3], 1), 1, 3).astype(jnp.int32)
    return {"user_factors": user_factors, "item_factors": item_factors, "obs_items": obs_items, "obs_conf": obs_conf}


LEARN_RATE = 0.0005
CONF_SCALE = 0.5
RIDGE_COEF = 0.01


def dense_counts(obs_rows, conf_rows, slab_rows):
    columns = lax.broadcasted_iota(jnp.int32, (1, 1, slab_rows), 2)
    hits = jnp.where(obs_rows[:, :, None] == columns, conf_rows[:, :, None].astype(jnp.float32), jnp.float32(0.0))
    return jnp.sum(hits, axis=1)


def block_step(user_rows, held, counts):
    scores = lax.dot_general(user_rows, held, (((1,), (1,)), ((), ())), precision=lax.Precision.HIGHEST, preferred_element_type=jnp.float32)
    target = jnp.where(counts > 0, 1.0, 0.0).astype(jnp.float32)
    weights = 1.0 + CONF_SCALE * counts
    errors = weights * (scores - target)
    grad_user = jnp.dot(errors, held, precision=lax.Precision.HIGHEST, preferred_element_type=jnp.float32) + RIDGE_COEF * user_rows
    partial_grad = lax.dot_general(errors, user_rows, (((0,), (0,)), ((), ())), precision=lax.Precision.HIGHEST, preferred_element_type=jnp.float32)
    return user_rows - LEARN_RATE * grad_user, partial_grad


def reference(user_factors, item_factors, obs_items, obs_conf):
    users_all = user_factors.reshape(N_BLK, U_DEV * N_SPLIT, R)
    held = item_factors.reshape(N_BLK, I_SLAB, R)
    items_all = obs_items.reshape(N_BLK, U_DEV * N_SPLIT, SUBS, OBS)
    conf_all = obs_conf.reshape(N_BLK, U_DEV * N_SPLIT, SUBS, OBS)

    def one_block(operands):
        user_rows, slab, obs_rows, conf_rows = operands
        counts = dense_counts(obs_rows, conf_rows, I_SLAB)
        new_rows, partial_grad = block_step(user_rows, slab, counts)
        return new_rows, slab - LEARN_RATE * (partial_grad + RIDGE_COEF * slab)

    for step in range(SUBS):
        users_all, held = lax.map(one_block, (users_all, held, items_all[:, :, step, :], conf_all[:, :, step, :]))
        held = jnp.roll(held, -1, axis=0)
    return users_all.reshape(USERS, R), held.reshape(ITEMS, R)
```

```python
import functools

import jax
import jax.numpy as jnp
from jax import lax
from jax.experimental import pallas as pl
from jax.experimental.pallas import tpu as pltpu
from jax.sharding import PartitionSpec as P

SUBS = 4


LEARN_RATE = 0.0005
CONF_SCALE = 0.5
RIDGE_COEF = 0.01

MESH = pl.DeviceIdType.MESH
PIECES = 2
COLS = 2


def halves(x):
    high = x.astype(jnp.bfloat16)
    return high, (x - high.astype(jnp.float32)).astype(jnp.bfloat16)


def product(a, b, dims):
    dot = functools.partial(
        lax.dot_general, dimension_numbers=(dims, ((), ())), preferred_element_type=jnp.float32
    )
    return dot(a[0], b[0]) + (dot(a[0], b[1]) + dot(a[1], b[0]))


BOTH_LAST = ((1,), (1,))
PLAIN = ((1,), (0,))
BOTH_FIRST = ((0,), (0,))


def kernel(
    n_blk, n_split,
    u_ref, h_ref, item_ref, conf_ref, u_out, i_out,
    users, users_hi, users_lo, slab_hi, slab_lo, err_hi, err_lo, counts, grad, item_in, conf_in,
    held, outgoing, share_in, share_buf,
    obs_send, obs_recv, u_send, u_recv, h_send, h_recv, share_send, share_recv,
):
    u_dev, rank = u_ref.shape
    slab_rows = h_ref.shape[0]
    share_rows = slab_rows // n_split
    piece = u_dev // PIECES
    col = rank // COLS
    blk = lax.axis_index("blk")
    spl = lax.axis_index("split")
    ahead = lax.rem(blk + n_blk - 1, n_blk)
    behind = lax.rem(blk + 1, n_blk)
    peers = [lax.rem(spl + q, n_split) for q in range(n_split)]
    share_at = pl.multiple_of(spl * share_rows, share_rows)

    barrier = pltpu.get_barrier_semaphore()
    for other in (ahead, behind):
        pl.semaphore_signal(barrier, inc=1, device_id=(other, spl), device_id_type=MESH)
    for q in range(1, n_split):
        pl.semaphore_signal(barrier, inc=1, device_id=(blk, peers[q]), device_id_type=MESH)
    pl.semaphore_wait(barrier, n_split + 1)

    obs_copies, user_copies = [None], [None]
    for q in range(1, n_split):
        slot = n_split - q
        copies = []
        for i, (here, there) in enumerate(((item_ref, item_in), (conf_ref, conf_in))):
            copy = pltpu.make_async_remote_copy(
                src_ref=here, dst_ref=there.at[slot - 1],
                send_sem=obs_send.at[q - 1, i], recv_sem=obs_recv.at[slot - 1, i],
                device_id=(blk, peers[q]), device_id_type=MESH,
            )
            copy.start()
            copies.append(copy)
        obs_copies.append(copies)
    for q in range(1, n_split):
        slot = n_split - q
        copies = []
        for p in range(PIECES):
            copy = pltpu.make_async_remote_copy(
                src_ref=u_ref.at[pl.ds(p * piece, piece)],
                dst_ref=users.at[pl.ds(slot * u_dev + p * piece, piece)],
                send_sem=u_send.at[q - 1, p], recv_sem=u_recv.at[slot - 1, p],
                device_id=(blk, peers[q]), device_id_type=MESH,
            )
            copy.start()
            copies.append(copy)
        user_copies.append(copies)

    def count(items, confs, q):
        rows = lax.broadcasted_iota(jnp.int32, (slab_rows, u_dev), 0)
        for step in range(SUBS):
            total = jnp.zeros((slab_rows, u_dev), jnp.float32)
            for k in range(items.shape[1]):
                conf = confs[step, k:k + 1, :].astype(jnp.float32)
                total = total + jnp.where(rows == items[step, k:k + 1, :], conf, 0.0)
            counts[step, :, q * u_dev:(q + 1) * u_dev] = total

    def errors(scores, r):
        target = jnp.where(r > 0, 1.0, 0.0).astype(jnp.float32)
        return (1.0 + CONF_SCALE * r) * (scores - target)

    def split_users(rows):
        high, low = halves(users[rows, :])
        users_hi[rows, :] = high
        users_lo[rows, :] = low

    def split_slab(slab, columns):
        high, low = halves(slab[:, columns])
        slab_hi[:, columns] = high
        slab_lo[:, columns] = low

    def scores_of(rows):
        return product(
            (slab_hi[...], slab_lo[...]), (users_hi[rows, :], users_lo[rows, :]), BOTH_LAST
        )

    def keep_errors(step, rows, scores):
        high, low = halves(errors(scores, counts[step, :, rows]))
        err_hi[:, rows] = high
        err_lo[:, rows] = low

    def item_grad(rows, columns):
        return product(
            (err_hi[:, rows], err_lo[:, rows]),
            (users_hi[rows, columns], users_lo[rows, columns]),
            PLAIN,
        )

    def user_step(rows):
        grad_user = product(
            (err_hi[:, rows], err_lo[:, rows]), (slab_hi[...], slab_lo[...]), BOTH_FIRST
        )
        old = users[rows, :]
        return old - LEARN_RATE * (grad_user + RIDGE_COEF * old)

    def send_slab(step, slab, c, total):
        columns = slice(c * col, (c + 1) * col)
        old = slab[:, columns]
        outgoing[step, c] = old - LEARN_RATE * (total + RIDGE_COEF * old)
        copy = pltpu.make_async_remote_copy(
            src_ref=outgoing.at[step, c], dst_ref=held.at[step, :, pl.ds(c * col, col)],
            send_sem=h_send.at[step, c], recv_sem=h_recv.at[step, c],
            device_id=(ahead, spl), device_id_type=MESH,
        )
        copy.start()
        return copy

    every = slice(0, n_split * u_dev)
    own = slice(0, u_dev)
    slab_copies = []

    users[own, :] = u_ref[...]
    split_users(own)
    split_slab(h_ref, slice(0, rank))
    count(item_ref, conf_ref, 0)
    keep_errors(0, own, scores_of(own))
    grad[...] = item_grad(own, slice(0, rank))
    for q in range(1, n_split):
        for copy in obs_copies[n_split - q]:
            copy.wait_recv()
        count(item_in.at[q - 1], conf_in.at[q - 1], q)
    for q in range(1, n_split):
        for p in range(PIECES):
            user_copies[n_split - q][p].wait_recv()
            rows = slice(q * u_dev + p * piece, q * u_dev + (p + 1) * piece)
            split_users(rows)
            keep_errors(0, rows, scores_of(rows))
            if q < n_split - 1 or p < PIECES - 1:
                grad[...] += item_grad(rows, slice(0, rank))
    for c in range(COLS):
        columns = slice(c * col, (c + 1) * col)
        total = grad[:, columns] + item_grad(rows, columns)
        slab_copies.append(send_slab(0, h_ref, c, total))

    def update_users():
        for q in range(n_split):
            rows = slice(q * u_dev, (q + 1) * u_dev)
            users[rows, :] = user_step(rows)
            split_users(rows)

    update_users()

    for step in range(1, SUBS):
        slab = held.at[step - 1]
        last = step == SUBS - 1
        for c in range(COLS):
            slab_copies[(step - 1) * COLS + c].wait_recv()
            split_slab(slab, slice(c * col, (c + 1) * col))
        if not last:
            keep_errors(step, every, scores_of(every))
            for c in range(COLS):
                columns = slice(c * col, (c + 1) * col)
                slab_copies.append(send_slab(step, slab, c, item_grad(every, columns)))
            update_users()
        else:
            keep_errors(step, own, scores_of(own))
            share = pl.ds(share_at, share_rows)
            total = product(
                (err_hi[share, own], err_lo[share, own]),
                (users_hi[own, :], users_lo[own, :]),
                PLAIN,
            )
            others = slice(u_dev, n_split * u_dev)
            scores = product(
                (slab_hi[share, :], slab_lo[share, :]),
                (users_hi[others, :], users_lo[others, :]),
                BOTH_LAST,
            )
            total = total + product(
                halves(errors(scores, counts[step, share, others])),
                (users_hi[others, :], users_lo[others, :]),
                PLAIN,
            )
            old = slab[share, :]
            share_buf[...] = old - LEARN_RATE * (total + RIDGE_COEF * old)
            share_copy = pltpu.make_async_remote_copy(
                src_ref=share_buf, dst_ref=share_in, send_sem=share_send, recv_sem=share_recv,
                device_id=(ahead, spl), device_id_type=MESH,
            )
            share_copy.start()
            u_out[...] = user_step(own)
    for q in range(1, n_split):
        for copy in obs_copies[q]:
            copy.wait_send()
        for p in range(PIECES):
            user_copies[q][p].wait_send()
    for slab_copy in slab_copies:
        slab_copy.wait_send()
    share_copy.wait_send()
    share_copy.wait_recv()
    i_out[...] = share_in[...]


def local(n_blk, n_split, user_factors, item_factors, obs_items, obs_conf):
    u_dev, rank = user_factors.shape
    slab_rows = item_factors.shape[0]
    share_rows = slab_rows // n_split
    subs = obs_items.shape[1]
    items, confs = (obs.transpose(1, 2, 0) for obs in (obs_items, obs_conf))
    everyone = n_split * u_dev
    f32, b16 = jnp.float32, jnp.bfloat16
    dma = pltpu.SemaphoreType.DMA
    return pl.pallas_call(
        functools.partial(kernel, n_blk, n_split),
        out_shape=(
            jax.ShapeDtypeStruct((u_dev, rank), f32),
            jax.ShapeDtypeStruct((share_rows, rank), f32),
        ),
        in_specs=[pl.BlockSpec(memory_space=pltpu.VMEM)] * 4,
        out_specs=(pl.BlockSpec(memory_space=pltpu.VMEM),) * 2,
        scratch_shapes=[
            pltpu.VMEM((everyone, rank), f32),
            pltpu.VMEM((everyone, rank), b16),
            pltpu.VMEM((everyone, rank), b16),
            pltpu.VMEM((slab_rows, rank), b16),
            pltpu.VMEM((slab_rows, rank), b16),
            pltpu.VMEM((slab_rows, everyone), b16),
            pltpu.VMEM((slab_rows, everyone), b16),
            pltpu.VMEM((subs, slab_rows, everyone), f32),
            pltpu.VMEM((slab_rows, rank), f32),
            pltpu.VMEM((n_split - 1,) + items.shape, jnp.int32),
            pltpu.VMEM((n_split - 1,) + items.shape, jnp.int32),
            pltpu.VMEM((subs - 1, slab_rows, rank), f32),
            pltpu.VMEM((subs - 1, COLS, slab_rows, rank // COLS), f32),
            pltpu.VMEM((share_rows, rank), f32),
            pltpu.VMEM((share_rows, rank), f32),
            dma((n_split - 1, 2)),
            dma((n_split - 1, 2)),
            dma((n_split - 1, PIECES)),
            dma((n_split - 1, PIECES)),
            dma((subs - 1, COLS)),
            dma((subs - 1, COLS)),
            dma,
            dma,
        ],
        compiler_params=pltpu.CompilerParams(
            collective_id=0, has_side_effects=True, vmem_limit_bytes=48 * 2**20
        ),
    )(user_factors, item_factors, items, confs)


def solution(mesh):
    in_specs = (
        P(("blk", "split"), None),
        P("blk", None),
        P(("blk", "split"), None, None),
        P(("blk", "split"), None, None),
    )
    out_specs = (P(("blk", "split"), None), P(("blk", "split"), None))
    body = functools.partial(local, mesh.shape["blk"], mesh.shape["split"])
    return jax.shard_map(body, mesh=mesh, in_specs=in_specs, out_specs=out_specs, check_vma=False)
```

```python
import functools

import jax
import jax.numpy as jnp
from jax import lax
from jax.experimental import pallas as pl
from jax.experimental.pallas import tpu as pltpu
from jax.sharding import PartitionSpec as P

SUBS = 4


LEARN_RATE = 0.0005
CONF_SCALE = 0.5
RIDGE_COEF = 0.01

MESH = pl.DeviceIdType.MESH
PIECES = 2
COLS = 2


def halves(x):
    high = x.astype(jnp.bfloat16)
    return high, (x - high.astype(jnp.float32)).astype(jnp.bfloat16)


def dot(a, b, dims):
    return lax.dot_general(a, b, (dims, ((), ())), preferred_element_type=jnp.float32)


def stacked(a, b, dims):
    rows = a.shape[0] // 2
    both = dot(a, b[0], dims)
    return both[:rows] + (both[rows:] + dot(a[:rows], b[1], dims))


BOTH_LAST = ((1,), (1,))
PLAIN = ((1,), (0,))
BOTH_FIRST = ((0,), (0,))


def kernel(
    n_blk, n_split,
    u_hbm, h_hbm, item_hbm, conf_hbm, u_out, i_out,
    users, users_hi, users_lo, slab_16, err_16, counts, grad, item_in, conf_in,
    held, outgoing, share_buf,
    load_sem, obs_send, obs_recv, u_send, u_recv, h_send, h_recv, share_send, share_recv,
):
    u_dev, rank = u_hbm.shape
    slab_rows = h_hbm.shape[0]
    share_rows = slab_rows // n_split
    piece = u_dev // PIECES
    col = rank // COLS
    blk = lax.axis_index("blk")
    spl = lax.axis_index("split")
    ahead = lax.rem(blk + n_blk - 1, n_blk)
    behind = lax.rem(blk + 1, n_blk)
    peers = [lax.rem(spl + q, n_split) for q in range(n_split)]
    share_at = pl.multiple_of(spl * share_rows, share_rows)

    barrier = pltpu.get_barrier_semaphore()
    for q in range(1, n_split):
        pl.semaphore_signal(barrier, inc=1, device_id=(blk, peers[q]), device_id_type=MESH)
    for other in (ahead, behind):
        pl.semaphore_signal(barrier, inc=1, device_id=(other, spl), device_id_type=MESH)
    loads = [
        pltpu.make_async_copy(there, here, load_sem.at[i])
        for i, (there, here) in enumerate((
            (u_hbm, users.at[pl.ds(0, u_dev)]),
            (h_hbm, held.at[0]),
            (item_hbm, item_in.at[0]),
            (conf_hbm, conf_in.at[0]),
        ))
    ]
    for load in loads:
        load.start()
    pl.semaphore_wait(barrier, n_split + 1)

    def send_obs(q, part, steps):
        slot = n_split - q
        copies = []
        for i, (here, there) in enumerate(((item_hbm, item_in), (conf_hbm, conf_in))):
            copy = pltpu.make_async_remote_copy(
                src_ref=here.at[steps], dst_ref=there.at[slot, steps],
                send_sem=obs_send.at[q - 1, part, i], recv_sem=obs_recv.at[slot - 1, part, i],
                device_id=(blk, peers[q]), device_id_type=MESH,
            )
            copy.start()
            copies.append(copy)
        return copies

    first, rest = pl.ds(0, 1), pl.ds(1, SUBS - 1)
    first_obs = [None] + [send_obs(q, 0, first) for q in range(1, n_split)]
    user_copies = [None]
    for q in range(1, n_split):
        slot = n_split - q
        copies = []
        for p in range(PIECES):
            copy = pltpu.make_async_remote_copy(
                src_ref=u_hbm.at[pl.ds(p * piece, piece)],
                dst_ref=users.at[pl.ds(slot * u_dev + p * piece, piece)],
                send_sem=u_send.at[q - 1, p], recv_sem=u_recv.at[slot - 1, p],
                device_id=(blk, peers[q]), device_id_type=MESH,
            )
            copy.start()
            copies.append(copy)
        user_copies.append(copies)

    def count(q, steps):
        rows = lax.broadcasted_iota(jnp.int32, (slab_rows, u_dev), 0)
        for step in steps:
            total = jnp.zeros((slab_rows, u_dev), jnp.float32)
            for k in range(item_in.shape[2]):
                item = item_in[q, step, k:k + 1, :]
                conf = conf_in[q, step, k:k + 1, :].astype(jnp.float32)
                total = total + jnp.where(rows == item, conf, 0.0)
            counts[step, :, q * u_dev:(q + 1) * u_dev] = total

    def errors(scores, r):
        target = jnp.where(r > 0, 1.0, 0.0).astype(jnp.float32)
        return (1.0 + CONF_SCALE * r) * (scores - target)

    def split_users(rows):
        high, low = halves(users[rows, :])
        users_hi[rows, :] = high
        users_lo[rows, :] = low

    def split_slab(slab, columns):
        high, low = halves(slab[:, columns])
        slab_16[0:slab_rows, columns] = high
        slab_16[slab_rows:2 * slab_rows, columns] = low
        slab_16[2 * slab_rows:, columns] = high

    def scores_of(rows, columns):
        return stacked(
            slab_16[0:2 * slab_rows, columns],
            (users_hi[rows, columns], users_lo[rows, columns]),
            BOTH_LAST,
        )

    def keep_errors(step, rows, scores):
        high, low = halves(errors(scores, counts[step, :, rows]))
        err_16[0:slab_rows, rows] = high
        err_16[slab_rows:2 * slab_rows, rows] = high
        err_16[2 * slab_rows:, rows] = low

    def item_grad(rows, columns):
        return stacked(
            err_16[slab_rows:, rows], (users_hi[rows, columns], users_lo[rows, columns]), PLAIN
        )

    def user_step(rows):
        grad_user = dot(err_16[:, rows], slab_16[...], BOTH_FIRST)
        old = users[rows, :]
        return old - LEARN_RATE * (grad_user + RIDGE_COEF * old)

    def send_slab(step, c, total):
        columns = slice(c * col, (c + 1) * col)
        old = held[step, :, columns]
        outgoing[step, c] = old - LEARN_RATE * (total + RIDGE_COEF * old)
        copy = pltpu.make_async_remote_copy(
            src_ref=outgoing.at[step, c], dst_ref=held.at[step + 1, :, pl.ds(c * col, col)],
            send_sem=h_send.at[step, c], recv_sem=h_recv.at[step, c],
            device_id=(ahead, spl), device_id_type=MESH,
        )
        copy.start()
        return copy

    whole = slice(0, rank)
    every = slice(0, n_split * u_dev)
    own = slice(0, u_dev)
    columns_of = [slice(c * col, (c + 1) * col) for c in range(COLS)]
    slab_copies = []

    for load in loads:
        load.wait()
    split_users(own)
    split_slab(held.at[0], whole)
    count(0, range(SUBS))
    keep_errors(0, own, scores_of(own, whole))
    grad[...] = item_grad(own, whole)
    for q in range(1, n_split):
        for copy in first_obs[n_split - q]:
            copy.wait_recv()
        count(q, range(1))
    rest_obs = [None]
    for q in range(1, n_split):
        for p in range(PIECES):
            user_copies[n_split - q][p].wait_recv()
            rows = slice(q * u_dev + p * piece, q * u_dev + (p + 1) * piece)
            split_users(rows)
            keep_errors(0, rows, scores_of(rows, whole))
            if q < n_split - 1 or p < PIECES - 1:
                grad[...] += item_grad(rows, whole)
    for c, columns in enumerate(columns_of):
        slab_copies.append(send_slab(0, c, grad[:, columns] + item_grad(rows, columns)))
    for q in range(1, n_split):
        rest_obs.append(send_obs(q, 1, rest))

    def update_users():
        for q in range(n_split):
            rows = slice(q * u_dev, (q + 1) * u_dev)
            users[rows, :] = user_step(rows)
            split_users(rows)

    update_users()
    for q in range(1, n_split):
        for copy in rest_obs[n_split - q]:
            copy.wait_recv()
        count(q, range(1, SUBS))

    for step in range(1, SUBS - 1):
        scores = 0.0
        for c, columns in enumerate(columns_of):
            slab_copies[(step - 1) * COLS + c].wait_recv()
            split_slab(held.at[step], columns)
            scores = scores + scores_of(every, columns)
        keep_errors(step, every, scores)
        for c, columns in enumerate(columns_of):
            slab_copies.append(send_slab(step, c, item_grad(every, columns)))
        update_users()

    last = SUBS - 1
    share = pl.ds(share_at, share_rows)
    low_share = pl.ds(pl.multiple_of(slab_rows + share_at, share_rows), share_rows)
    scores = 0.0
    for c, columns in enumerate(columns_of):
        slab_copies[(last - 1) * COLS + c].wait_recv()
        split_slab(held.at[last], columns)
        scores = scores + stacked(
            jnp.concatenate([slab_16[share, columns], slab_16[low_share, columns]], axis=0),
            (users_hi[:, columns], users_lo[:, columns]),
            BOTH_LAST,
        )
    share_errors = jnp.concatenate(halves(errors(scores, counts[last, share, :])), axis=0)
    total = stacked(share_errors, (users_hi[...], users_lo[...]), PLAIN)
    old = held[last, share, :]
    share_buf[...] = old - LEARN_RATE * (total + RIDGE_COEF * old)
    share_copy = pltpu.make_async_remote_copy(
        src_ref=share_buf, dst_ref=i_out, send_sem=share_send, recv_sem=share_recv,
        device_id=(ahead, spl), device_id_type=MESH,
    )
    share_copy.start()
    keep_errors(last, own, scores_of(own, whole))
    users[own, :] = user_step(own)
    store = pltpu.make_async_copy(users.at[pl.ds(0, u_dev)], u_out, load_sem.at[0])
    store.start()

    for q in range(1, n_split):
        for copy in first_obs[q] + rest_obs[q] + user_copies[q]:
            copy.wait_send()
    for copy in slab_copies:
        copy.wait_send()
    share_copy.wait_send()
    share_copy.wait_recv()
    store.wait()


def local(n_blk, n_split, user_factors, item_factors, obs_items, obs_conf):
    u_dev, rank = user_factors.shape
    slab_rows = item_factors.shape[0]
    share_rows = slab_rows // n_split
    subs = obs_items.shape[1]
    items, confs = (obs.transpose(1, 2, 0) for obs in (obs_items, obs_conf))
    everyone = n_split * u_dev
    f32, b16 = jnp.float32, jnp.bfloat16
    dma = pltpu.SemaphoreType.DMA
    return pl.pallas_call(
        functools.partial(kernel, n_blk, n_split),
        out_shape=(
            jax.ShapeDtypeStruct((u_dev, rank), f32),
            jax.ShapeDtypeStruct((share_rows, rank), f32),
        ),
        in_specs=[pl.BlockSpec(memory_space=pltpu.HBM)] * 4,
        out_specs=(pl.BlockSpec(memory_space=pl.ANY),) * 2,
        scratch_shapes=[
            pltpu.VMEM((everyone, rank), f32),
            pltpu.VMEM((everyone, rank), b16),
            pltpu.VMEM((everyone, rank), b16),
            pltpu.VMEM((3 * slab_rows, rank), b16),
            pltpu.VMEM((3 * slab_rows, everyone), b16),
            pltpu.VMEM((subs, slab_rows, everyone), f32),
            pltpu.VMEM((slab_rows, rank), f32),
            pltpu.VMEM((n_split,) + items.shape, jnp.int32),
            pltpu.VMEM((n_split,) + items.shape, jnp.int32),
            pltpu.VMEM((subs, slab_rows, rank), f32),
            pltpu.VMEM((subs - 1, COLS, slab_rows, rank // COLS), f32),
            pltpu.VMEM((share_rows, rank), f32),
            dma((4,)),
            dma((n_split - 1, 2, 2)),
            dma((n_split - 1, 2, 2)),
            dma((n_split - 1, PIECES)),
            dma((n_split - 1, PIECES)),
            dma((subs - 1, COLS)),
            dma((subs - 1, COLS)),
            dma,
            dma,
        ],
        compiler_params=pltpu.CompilerParams(
            collective_id=0, has_side_effects=True, vmem_limit_bytes=63 * 2**20
        ),
    )(user_factors, item_factors, items, confs)


def solution(mesh):
    in_specs = (
        P(("blk", "split"), None),
        P("blk", None),
        P(("blk", "split"), None, None),
        P(("blk", "split"), None, None),
    )
    out_specs = (P(("blk", "split"), None), P(("blk", "split"), None))
    body = functools.partial(local, mesh.shape["blk"], mesh.shape["split"])
    return jax.shard_map(body, mesh=mesh, in_specs=in_specs, out_specs=out_specs, check_vma=False)
```

```python
import functools

import jax
import jax.numpy as jnp
from jax import lax
from jax.experimental import pallas as pl
from jax.experimental.pallas import tpu as pltpu
from jax.sharding import PartitionSpec as P

SUBS = 4


LEARN_RATE = 0.0005
CONF_SCALE = 0.5
RIDGE_COEF = 0.01

MESH = pl.DeviceIdType.MESH
PIECES = 4
PARTS = 2
COLS = 2


def halves(x):
    high = x.astype(jnp.bfloat16)
    return high, (x - high.astype(jnp.float32)).astype(jnp.bfloat16)


def dot(a, b, dims):
    return lax.dot_general(a, b, (dims, ((), ())), preferred_element_type=jnp.float32)


def stacked(a, b, dims):
    rows = a.shape[0] // 2
    both = dot(a, b[0], dims)
    return both[:rows] + (both[rows:] + dot(a[:rows], b[1], dims))


BOTH_LAST = ((1,), (1,))
PLAIN = ((1,), (0,))
BOTH_FIRST = ((0,), (0,))


def kernel(
    n_blk, n_split,
    u_hbm, h_hbm, item_hbm, conf_hbm, u_out, i_out,
    users, users_hi, users_lo, slab_16, err_16, counts, grad, item_in, conf_in,
    held, outgoing, share_buf,
    load_sem, turn_sem, obs_send, obs_recv, u_send, u_recv, h_send, h_recv, share_send, share_recv,
):
    u_dev, rank = u_hbm.shape
    slab_rows = h_hbm.shape[0]
    share_rows = slab_rows // n_split
    piece = u_dev // PIECES
    col = rank // COLS
    blk = lax.axis_index("blk")
    spl = lax.axis_index("split")
    ahead = lax.rem(blk + n_blk - 1, n_blk)
    behind = lax.rem(blk + 1, n_blk)
    peers = [lax.rem(spl + q, n_split) for q in range(n_split)]
    share_at = pl.multiple_of(spl * share_rows, share_rows)

    barrier = pltpu.get_barrier_semaphore()
    for q in range(1, n_split):
        pl.semaphore_signal(barrier, inc=1, device_id=(blk, peers[q]), device_id_type=MESH)
    for other in (ahead, behind):
        pl.semaphore_signal(barrier, inc=1, device_id=(other, spl), device_id_type=MESH)
    loads = [
        pltpu.make_async_copy(there, here, load_sem.at[i])
        for i, (there, here) in enumerate((
            (u_hbm, users.at[pl.ds(0, u_dev)]),
            (h_hbm, held.at[0]),
            (item_hbm, item_in.at[0]),
            (conf_hbm, conf_in.at[0]),
        ))
    ]
    for load in loads:
        load.start()
    pl.semaphore_wait(barrier, n_split + 1)

    def send_obs(q, part, steps):
        slot = n_split - q
        copies = []
        for i, (here, there) in enumerate(((item_hbm, item_in), (conf_hbm, conf_in))):
            copy = pltpu.make_async_remote_copy(
                src_ref=here.at[steps], dst_ref=there.at[slot, steps],
                send_sem=obs_send.at[q - 1, part, i], recv_sem=obs_recv.at[slot - 1, part, i],
                device_id=(blk, peers[q]), device_id_type=MESH,
            )
            copy.start()
            copies.append(copy)
        return copies

    first, rest = pl.ds(0, 1), pl.ds(1, SUBS - 1)
    first_obs = [None] + [send_obs(q, 0, first) for q in range(1, n_split)]
    user_copies = [None] + [
        [
            pltpu.make_async_remote_copy(
                src_ref=u_hbm.at[pl.ds(p * piece, piece)],
                dst_ref=users.at[pl.ds((n_split - q) * u_dev + p * piece, piece)],
                send_sem=u_send.at[q - 1, p], recv_sem=u_recv.at[n_split - q - 1, p],
                device_id=(blk, peers[q]), device_id_type=MESH,
            )
            for p in range(PIECES)
        ]
        for q in range(1, n_split)
    ]

    def send_users():
        for q in range(1, n_split):
            for copy in user_copies[q]:
                copy.start()

    paired = n_blk % 2 == 0
    even = lax.rem(blk, 2) == 0 if paired else blk >= 0
    pl.when(even)(send_users)

    def count(q, steps):
        rows = lax.broadcasted_iota(jnp.int32, (slab_rows, u_dev), 0)
        for step in steps:
            total = jnp.zeros((slab_rows, u_dev), jnp.float32)
            for k in range(item_in.shape[2]):
                item = item_in[q, step, k:k + 1, :]
                conf = conf_in[q, step, k:k + 1, :].astype(jnp.float32)
                total = total + jnp.where(rows == item, conf, 0.0)
            counts[step, :, q * u_dev:(q + 1) * u_dev] = total

    def errors(scores, r):
        target = jnp.where(r > 0, 1.0, 0.0).astype(jnp.float32)
        return (1.0 + CONF_SCALE * r) * (scores - target)

    def split_users(rows):
        high, low = halves(users[rows, :])
        users_hi[rows, :] = high
        users_lo[rows, :] = low

    def split_slab(slab, columns):
        high, low = halves(slab[:, columns])
        slab_16[0:slab_rows, columns] = high
        slab_16[slab_rows:2 * slab_rows, columns] = low
        slab_16[2 * slab_rows:, columns] = high

    def scores_of(rows, columns):
        return stacked(
            slab_16[0:2 * slab_rows, columns],
            (users_hi[rows, columns], users_lo[rows, columns]),
            BOTH_LAST,
        )

    def keep_errors(step, rows, scores):
        high, low = halves(errors(scores, counts[step, :, rows]))
        err_16[0:slab_rows, rows] = high
        err_16[slab_rows:2 * slab_rows, rows] = high
        err_16[2 * slab_rows:, rows] = low

    def item_grad(rows, columns):
        return stacked(
            err_16[slab_rows:, rows], (users_hi[rows, columns], users_lo[rows, columns]), PLAIN
        )

    def user_step(rows):
        grad_user = dot(err_16[:, rows], slab_16[...], BOTH_FIRST)
        old = users[rows, :]
        return old - LEARN_RATE * (grad_user + RIDGE_COEF * old)

    def send_slab(step, c, total):
        columns = slice(c * col, (c + 1) * col)
        old = held[step, :, columns]
        outgoing[step, c] = old - LEARN_RATE * (total + RIDGE_COEF * old)
        copy = pltpu.make_async_remote_copy(
            src_ref=outgoing.at[step, c], dst_ref=held.at[step + 1, :, pl.ds(c * col, col)],
            send_sem=h_send.at[step, c], recv_sem=h_recv.at[step, c],
            device_id=(ahead, spl), device_id_type=MESH,
        )
        copy.start()
        return copy

    whole = slice(0, rank)
    every = slice(0, n_split * u_dev)
    own = slice(0, u_dev)
    columns_of = [slice(c * col, (c + 1) * col) for c in range(COLS)]
    slab_copies = []

    for load in loads:
        load.wait()
    split_users(own)
    split_slab(held.at[0], whole)
    count(0, range(SUBS))
    keep_errors(0, own, scores_of(own, whole))
    grad[...] = item_grad(own, whole)
    for q in range(1, n_split):
        for copy in first_obs[n_split - q]:
            copy.wait_recv()
        count(q, range(1))
    if paired:

        @pl.when(jnp.logical_not(even))
        def _():
            pl.semaphore_wait(turn_sem, 1)
            send_users()

    rest_obs = [None]
    part = u_dev // PARTS
    for q in range(1, n_split):
        for p in range(PIECES):
            user_copies[n_split - q][p].wait_recv()
            if paired and q == n_split - 1 and p == PIECES - 2:

                @pl.when(even)
                def _():
                    pl.semaphore_signal(
                        turn_sem, inc=1, device_id=(behind, spl), device_id_type=MESH
                    )

            done = (p + 1) * piece
            if done % part == 0:
                rows = slice(q * u_dev + done - part, q * u_dev + done)
                split_users(rows)
                keep_errors(0, rows, scores_of(rows, whole))
                if q < n_split - 1 or p < PIECES - 1:
                    grad[...] += item_grad(rows, whole)
    for c, columns in enumerate(columns_of):
        slab_copies.append(send_slab(0, c, grad[:, columns] + item_grad(rows, columns)))
    for q in range(1, n_split):
        rest_obs.append(send_obs(q, 1, rest))

    def update_users():
        for q in range(n_split):
            rows = slice(q * u_dev, (q + 1) * u_dev)
            users[rows, :] = user_step(rows)
            split_users(rows)

    update_users()
    for q in range(1, n_split):
        for copy in rest_obs[n_split - q]:
            copy.wait_recv()
        count(q, range(1, SUBS))

    for step in range(1, SUBS - 1):
        scores = 0.0
        for c, columns in enumerate(columns_of):
            slab_copies[(step - 1) * COLS + c].wait_recv()
            split_slab(held.at[step], columns)
            scores = scores + scores_of(every, columns)
        keep_errors(step, every, scores)
        for c, columns in enumerate(columns_of):
            slab_copies.append(send_slab(step, c, item_grad(every, columns)))
        update_users()

    last = SUBS - 1
    share = pl.ds(share_at, share_rows)
    low_share = pl.ds(pl.multiple_of(slab_rows + share_at, share_rows), share_rows)
    scores = 0.0
    for c, columns in enumerate(columns_of):
        slab_copies[(last - 1) * COLS + c].wait_recv()
        split_slab(held.at[last], columns)
        scores = scores + stacked(
            jnp.concatenate([slab_16[share, columns], slab_16[low_share, columns]], axis=0),
            (users_hi[:, columns], users_lo[:, columns]),
            BOTH_LAST,
        )
    share_errors = jnp.concatenate(halves(errors(scores, counts[last, share, :])), axis=0)
    total = stacked(share_errors, (users_hi[...], users_lo[...]), PLAIN)
    old = held[last, share, :]
    share_buf[...] = old - LEARN_RATE * (total + RIDGE_COEF * old)
    share_copy = pltpu.make_async_remote_copy(
        src_ref=share_buf, dst_ref=i_out, send_sem=share_send, recv_sem=share_recv,
        device_id=(ahead, spl), device_id_type=MESH,
    )
    share_copy.start()
    keep_errors(last, own, scores_of(own, whole))
    users[own, :] = user_step(own)
    store = pltpu.make_async_copy(users.at[pl.ds(0, u_dev)], u_out, load_sem.at[0])
    store.start()

    for q in range(1, n_split):
        for copy in first_obs[q] + rest_obs[q] + user_copies[q]:
            copy.wait_send()
    for copy in slab_copies:
        copy.wait_send()
    share_copy.wait_send()
    share_copy.wait_recv()
    store.wait()


def store_kernel(u_in, i_in, u_out, i_out, sems):
    copies = [
        pltpu.make_async_copy(u_in, u_out, sems.at[0]),
        pltpu.make_async_copy(i_in, i_out, sems.at[1]),
    ]
    for copy in copies:
        copy.start()
    for copy in copies:
        copy.wait()


def local(n_blk, n_split, user_factors, item_factors, obs_items, obs_conf):
    u_dev, rank = user_factors.shape
    slab_rows = item_factors.shape[0]
    share_rows = slab_rows // n_split
    subs = obs_items.shape[1]
    items, confs = (obs.transpose(1, 2, 0) for obs in (obs_items, obs_conf))
    everyone = n_split * u_dev
    f32, b16 = jnp.float32, jnp.bfloat16
    dma = pltpu.SemaphoreType.DMA
    results = pl.pallas_call(
        functools.partial(kernel, n_blk, n_split),
        out_shape=(
            jax.ShapeDtypeStruct((u_dev, rank), f32),
            jax.ShapeDtypeStruct((share_rows, rank), f32),
        ),
        in_specs=[pl.BlockSpec(memory_space=pltpu.HBM)] * 4,
        out_specs=(pl.BlockSpec(memory_space=pl.ANY),) * 2,
        scratch_shapes=[
            pltpu.VMEM((everyone, rank), f32),
            pltpu.VMEM((everyone, rank), b16),
            pltpu.VMEM((everyone, rank), b16),
            pltpu.VMEM((3 * slab_rows, rank), b16),
            pltpu.VMEM((3 * slab_rows, everyone), b16),
            pltpu.VMEM((subs, slab_rows, everyone), f32),
            pltpu.VMEM((slab_rows, rank), f32),
            pltpu.VMEM((n_split,) + items.shape, jnp.int32),
            pltpu.VMEM((n_split,) + items.shape, jnp.int32),
            pltpu.VMEM((subs, slab_rows, rank), f32),
            pltpu.VMEM((subs - 1, COLS, slab_rows, rank // COLS), f32),
            pltpu.VMEM((share_rows, rank), f32),
            dma((4,)),
            pltpu.SemaphoreType.REGULAR,
            dma((n_split - 1, 2, 2)),
            dma((n_split - 1, 2, 2)),
            dma((n_split - 1, PIECES)),
            dma((n_split - 1, PIECES)),
            dma((subs - 1, COLS)),
            dma((subs - 1, COLS)),
            dma,
            dma,
        ],
        compiler_params=pltpu.CompilerParams(
            collective_id=0, has_side_effects=True, vmem_limit_bytes=63 * 2**20
        ),
    )(user_factors, item_factors, items, confs)
    return pl.pallas_call(
        store_kernel,
        out_shape=tuple(jax.ShapeDtypeStruct(x.shape, x.dtype) for x in results),
        in_specs=[pl.BlockSpec(memory_space=pl.ANY)] * 2,
        out_specs=(pl.BlockSpec(memory_space=pl.ANY),) * 2,
        scratch_shapes=[dma((2,))],
        compiler_params=pltpu.CompilerParams(vmem_limit_bytes=63 * 2**20),
    )(*results)


def solution(mesh):
    in_specs = (
        P(("blk", "split"), None),
        P("blk", None),
        P(("blk", "split"), None, None),
        P(("blk", "split"), None, None),
    )
    out_specs = (P(("blk", "split"), None), P(("blk", "split"), None))
    body = functools.partial(local, mesh.shape["blk"], mesh.shape["split"])
    return jax.shard_map(body, mesh=mesh, in_specs=in_specs, out_specs=out_specs, check_vma=False)
```

```python
import functools

import jax
import jax.numpy as jnp
from jax import lax
from jax.experimental import pallas as pl
from jax.experimental.pallas import tpu as pltpu
from jax.sharding import PartitionSpec as P

SUBS = 4


LEARN_RATE = 0.0005
CONF_SCALE = 0.5
RIDGE_COEF = 0.01

MESH = pl.DeviceIdType.MESH
PIECES = 4
PARTS = 2
COLS = 2


def halves(x):
    high = x.astype(jnp.bfloat16)
    return high, (x - high.astype(jnp.float32)).astype(jnp.bfloat16)


def dot(a, b, dims):
    return lax.dot_general(a, b, (dims, ((), ())), preferred_element_type=jnp.float32)


def stacked(a, b, dims):
    rows = a.shape[0] // 2
    both = dot(a, b[0], dims)
    return both[:rows] + (both[rows:] + dot(a[:rows], b[1], dims))


BOTH_LAST = ((1,), (1,))
PLAIN = ((1,), (0,))
BOTH_FIRST = ((0,), (0,))


def kernel(
    n_blk, n_split,
    u_hbm, h_hbm, item_hbm, conf_hbm, u_out, i_out,
    users, users_hi, users_lo, slab_16, err_16, counts, grad, item_in, conf_in,
    held, outgoing, share_buf,
    load_sem, turn_sem, obs_send, obs_recv, u_send, u_recv, h_send, h_recv, share_send, share_recv,
):
    u_dev, rank = u_hbm.shape
    slab_rows = h_hbm.shape[0]
    share_rows = slab_rows // n_split
    piece = u_dev // PIECES
    col = rank // COLS
    blk = lax.axis_index("blk")
    spl = lax.axis_index("split")
    ahead = lax.rem(blk + n_blk - 1, n_blk)
    behind = lax.rem(blk + 1, n_blk)
    peers = [lax.rem(spl + q, n_split) for q in range(n_split)]
    share_at = pl.multiple_of(spl * share_rows, share_rows)

    barrier = pltpu.get_barrier_semaphore()
    for q in range(1, n_split):
        pl.semaphore_signal(barrier, inc=1, device_id=(blk, peers[q]), device_id_type=MESH)
    for other in (ahead, behind):
        pl.semaphore_signal(barrier, inc=1, device_id=(other, spl), device_id_type=MESH)
    loads = [
        pltpu.make_async_copy(there, here, load_sem.at[i])
        for i, (there, here) in enumerate((
            (u_hbm, users.at[pl.ds(0, u_dev)]),
            (item_hbm, item_in.at[0]),
            (conf_hbm, conf_in.at[0]),
            *((h_hbm.at[:, pl.ds(c * col, col)], held.at[0, c]) for c in range(COLS)),
        ))
    ]
    for load in loads:
        load.start()
    pl.semaphore_wait(barrier, n_split + 1)

    def send_obs(q, part, steps):
        slot = n_split - q
        copies = []
        for i, (here, there) in enumerate(((item_hbm, item_in), (conf_hbm, conf_in))):
            copy = pltpu.make_async_remote_copy(
                src_ref=here.at[steps], dst_ref=there.at[slot, steps],
                send_sem=obs_send.at[q - 1, part, i], recv_sem=obs_recv.at[slot - 1, part, i],
                device_id=(blk, peers[q]), device_id_type=MESH,
            )
            copy.start()
            copies.append(copy)
        return copies

    first, rest = pl.ds(0, 1), pl.ds(1, SUBS - 1)
    first_obs = [None] + [send_obs(q, 0, first) for q in range(1, n_split)]
    user_copies = [None] + [
        [
            pltpu.make_async_remote_copy(
                src_ref=u_hbm.at[pl.ds(p * piece, piece)],
                dst_ref=users.at[pl.ds((n_split - q) * u_dev + p * piece, piece)],
                send_sem=u_send.at[q - 1, p], recv_sem=u_recv.at[n_split - q - 1, p],
                device_id=(blk, peers[q]), device_id_type=MESH,
            )
            for p in range(PIECES)
        ]
        for q in range(1, n_split)
    ]

    def send_users():
        for q in range(1, n_split):
            for copy in user_copies[q]:
                copy.start()

    paired = n_blk % 2 == 0
    even = lax.rem(blk, 2) == 0 if paired else blk >= 0
    pl.when(even)(send_users)

    def count(q, steps):
        rows = lax.broadcasted_iota(jnp.int32, (slab_rows, u_dev), 0)
        for step in steps:
            total = jnp.zeros((slab_rows, u_dev), jnp.float32)
            for k in range(item_in.shape[2]):
                item = item_in[q, step, k:k + 1, :]
                conf = conf_in[q, step, k:k + 1, :].astype(jnp.float32)
                total = total + jnp.where(rows == item, conf, 0.0)
            counts[step, :, q * u_dev:(q + 1) * u_dev] = total

    def errors(scores, r):
        target = jnp.where(r > 0, 1.0, 0.0).astype(jnp.float32)
        return (1.0 + CONF_SCALE * r) * (scores - target)

    def split_users(rows):
        high, low = halves(users[rows, :])
        users_hi[rows, :] = high
        users_lo[rows, :] = low

    def split_slab(step, c):
        columns = columns_of[c]
        high, low = halves(held[step, c])
        slab_16[0:slab_rows, columns] = high
        slab_16[slab_rows:2 * slab_rows, columns] = low
        slab_16[2 * slab_rows:, columns] = high

    def scores_of(rows, columns):
        return stacked(
            slab_16[0:2 * slab_rows, columns],
            (users_hi[rows, columns], users_lo[rows, columns]),
            BOTH_LAST,
        )

    def keep_errors(step, rows, scores):
        high, low = halves(errors(scores, counts[step, :, rows]))
        err_16[0:slab_rows, rows] = high
        err_16[slab_rows:2 * slab_rows, rows] = high
        err_16[2 * slab_rows:, rows] = low

    def item_grad(rows, columns):
        return stacked(
            err_16[slab_rows:, rows], (users_hi[rows, columns], users_lo[rows, columns]), PLAIN
        )

    def user_step(rows):
        grad_user = dot(err_16[:, rows], slab_16[...], BOTH_FIRST)
        old = users[rows, :]
        return old - LEARN_RATE * (grad_user + RIDGE_COEF * old)

    def send_slab(step, c, total):
        old = held[step, c]
        outgoing[step, c] = old - LEARN_RATE * (total + RIDGE_COEF * old)
        copy = pltpu.make_async_remote_copy(
            src_ref=outgoing.at[step, c], dst_ref=held.at[step + 1, c],
            send_sem=h_send.at[step, c], recv_sem=h_recv.at[step, c],
            device_id=(ahead, spl), device_id_type=MESH,
        )
        copy.start()
        return copy

    whole = slice(0, rank)
    every = slice(0, n_split * u_dev)
    own = slice(0, u_dev)
    columns_of = [slice(c * col, (c + 1) * col) for c in range(COLS)]
    slab_copies = []

    for load in loads:
        load.wait()
    split_users(own)
    for c in range(COLS):
        split_slab(0, c)
    count(0, range(SUBS))
    keep_errors(0, own, scores_of(own, whole))
    grad[...] = item_grad(own, whole)
    for q in range(1, n_split):
        for copy in first_obs[n_split - q]:
            copy.wait_recv()
        count(q, range(1))
    if paired:

        @pl.when(jnp.logical_not(even))
        def _():
            pl.semaphore_wait(turn_sem, 1)
            send_users()

    rest_obs = [None]
    part = u_dev // PARTS
    for q in range(1, n_split):
        for p in range(PIECES):
            user_copies[n_split - q][p].wait_recv()
            if paired and q == n_split - 1 and p == PIECES - 2:

                @pl.when(even)
                def _():
                    pl.semaphore_signal(
                        turn_sem, inc=1, device_id=(behind, spl), device_id_type=MESH
                    )

            done = (p + 1) * piece
            if done % part == 0:
                rows = slice(q * u_dev + done - part, q * u_dev + done)
                split_users(rows)
                keep_errors(0, rows, scores_of(rows, whole))
                if q < n_split - 1 or p < PIECES - 1:
                    grad[...] += item_grad(rows, whole)
    for c, columns in enumerate(columns_of):
        slab_copies.append(send_slab(0, c, grad[:, columns] + item_grad(rows, columns)))
    for q in range(1, n_split):
        rest_obs.append(send_obs(q, 1, rest))

    def update_users():
        for q in range(n_split):
            rows = slice(q * u_dev, (q + 1) * u_dev)
            users[rows, :] = user_step(rows)
            split_users(rows)

    update_users()
    for q in range(1, n_split):
        for copy in rest_obs[n_split - q]:
            copy.wait_recv()
        count(q, range(1, SUBS))

    for step in range(1, SUBS - 1):
        scores = 0.0
        for c, columns in enumerate(columns_of):
            slab_copies[(step - 1) * COLS + c].wait_recv()
            split_slab(step, c)
            scores = scores + scores_of(every, columns)
        keep_errors(step, every, scores)
        for c, columns in enumerate(columns_of):
            slab_copies.append(send_slab(step, c, item_grad(every, columns)))
        update_users()

    last = SUBS - 1
    share = pl.ds(share_at, share_rows)
    low_share = pl.ds(pl.multiple_of(slab_rows + share_at, share_rows), share_rows)
    scores = 0.0
    for c, columns in enumerate(columns_of):
        slab_copies[(last - 1) * COLS + c].wait_recv()
        split_slab(last, c)
        scores = scores + stacked(
            jnp.concatenate([slab_16[share, columns], slab_16[low_share, columns]], axis=0),
            (users_hi[:, columns], users_lo[:, columns]),
            BOTH_LAST,
        )
    share_errors = jnp.concatenate(halves(errors(scores, counts[last, share, :])), axis=0)
    share_copies = []
    for c, columns in enumerate(columns_of):
        total = stacked(share_errors, (users_hi[:, columns], users_lo[:, columns]), PLAIN)
        old = held[last, c, share, :]
        share_buf[c] = old - LEARN_RATE * (total + RIDGE_COEF * old)
        copy = pltpu.make_async_remote_copy(
            src_ref=share_buf.at[c], dst_ref=i_out.at[:, pl.ds(c * col, col)],
            send_sem=share_send.at[c], recv_sem=share_recv.at[c],
            device_id=(ahead, spl), device_id_type=MESH,
        )
        copy.start()
        share_copies.append(copy)
    keep_errors(last, own, scores_of(own, whole))
    users[own, :] = user_step(own)
    store = pltpu.make_async_copy(users.at[pl.ds(0, u_dev)], u_out, load_sem.at[0])
    store.start()

    for q in range(1, n_split):
        for copy in first_obs[q] + rest_obs[q] + user_copies[q]:
            copy.wait_send()
    for copy in slab_copies:
        copy.wait_send()
    for copy in share_copies:
        copy.wait_send()
        copy.wait_recv()
    store.wait()


def store_kernel(u_in, i_in, u_out, i_out, u_buf, i_buf, load_sem, store_sem):
    rows = u_in.shape[0] // PIECES
    pieces = [(i_in, i_buf, i_out)]
    for p in range(PIECES):
        at = pl.ds(p * rows, rows)
        pieces.append((u_in.at[at], u_buf.at[at], u_out.at[at]))
    loads = [
        pltpu.make_async_copy(there, here, load_sem.at[i]) for i, (there, here, _) in enumerate(pieces)
    ]
    stores = [
        pltpu.make_async_copy(here, out, store_sem.at[i]) for i, (_, here, out) in enumerate(pieces)
    ]
    for load in loads:
        load.start()
    for load, store in zip(loads, stores):
        load.wait()
        store.start()
    for store in stores:
        store.wait()


def local(n_blk, n_split, user_factors, item_factors, obs_items, obs_conf):
    u_dev, rank = user_factors.shape
    slab_rows = item_factors.shape[0]
    share_rows = slab_rows // n_split
    subs = obs_items.shape[1]
    items, confs = (obs.transpose(1, 2, 0) for obs in (obs_items, obs_conf))
    everyone = n_split * u_dev
    f32, b16 = jnp.float32, jnp.bfloat16
    dma = pltpu.SemaphoreType.DMA
    results = pl.pallas_call(
        functools.partial(kernel, n_blk, n_split),
        out_shape=(
            jax.ShapeDtypeStruct((u_dev, rank), f32),
            jax.ShapeDtypeStruct((share_rows, rank), f32),
        ),
        in_specs=[pl.BlockSpec(memory_space=pltpu.HBM)] * 4,
        out_specs=(pl.BlockSpec(memory_space=pl.ANY),) * 2,
        scratch_shapes=[
            pltpu.VMEM((everyone, rank), f32),
            pltpu.VMEM((everyone, rank), b16),
            pltpu.VMEM((everyone, rank), b16),
            pltpu.VMEM((3 * slab_rows, rank), b16),
            pltpu.VMEM((3 * slab_rows, everyone), b16),
            pltpu.VMEM((subs, slab_rows, everyone), f32),
            pltpu.VMEM((slab_rows, rank), f32),
            pltpu.VMEM((n_split,) + items.shape, jnp.int32),
            pltpu.VMEM((n_split,) + items.shape, jnp.int32),
            pltpu.VMEM((subs, COLS, slab_rows, rank // COLS), f32),
            pltpu.VMEM((subs - 1, COLS, slab_rows, rank // COLS), f32),
            pltpu.VMEM((COLS, share_rows, rank // COLS), f32),
            dma((3 + COLS,)),
            pltpu.SemaphoreType.REGULAR,
            dma((n_split - 1, 2, 2)),
            dma((n_split - 1, 2, 2)),
            dma((n_split - 1, PIECES)),
            dma((n_split - 1, PIECES)),
            dma((subs - 1, COLS)),
            dma((subs - 1, COLS)),
            dma((COLS,)),
            dma((COLS,)),
        ],
        compiler_params=pltpu.CompilerParams(
            collective_id=0, has_side_effects=True, vmem_limit_bytes=63 * 2**20
        ),
    )(user_factors, item_factors, items, confs)
    return pl.pallas_call(
        store_kernel,
        out_shape=tuple(jax.ShapeDtypeStruct(x.shape, x.dtype) for x in results),
        in_specs=[pl.BlockSpec(memory_space=pl.ANY)] * 2,
        out_specs=(pl.BlockSpec(memory_space=pl.ANY),) * 2,
        scratch_shapes=[
            *(pltpu.VMEM(x.shape, x.dtype) for x in results),
            dma((PIECES + 1,)),
            dma((PIECES + 1,)),
        ],
        compiler_params=pltpu.CompilerParams(vmem_limit_bytes=63 * 2**20),
    )(*results)


def solution(mesh):
    in_specs = (
        P(("blk", "split"), None),
        P("blk", None),
        P(("blk", "split"), None, None),
        P(("blk", "split"), None, None),
    )
    out_specs = (P(("blk", "split"), None), P(("blk", "split"), None))
    body = functools.partial(local, mesh.shape["blk"], mesh.shape["split"])
    return jax.shard_map(body, mesh=mesh, in_specs=in_specs, out_specs=out_specs, check_vma=False)
```

```python
import functools

import jax
import jax.numpy as jnp
from jax import lax
from jax.experimental import pallas as pl
from jax.experimental.pallas import tpu as pltpu
from jax.sharding import PartitionSpec as P

SUBS = 4


LEARN_RATE = 0.0005
CONF_SCALE = 0.5
RIDGE_COEF = 0.01

MESH = pl.DeviceIdType.MESH
PIECES = 4
PARTS = 2
COLS = 2


def halves(x):
    high = x.astype(jnp.bfloat16)
    return high, (x - high.astype(jnp.float32)).astype(jnp.bfloat16)


def dot(a, b, dims):
    return lax.dot_general(a, b, (dims, ((), ())), preferred_element_type=jnp.float32)


def stacked(a, b, dims):
    rows = a.shape[0] // 2
    both = dot(a, b[0], dims)
    return both[:rows] + (both[rows:] + dot(a[:rows], b[1], dims))


BOTH_LAST = ((1,), (1,))
PLAIN = ((1,), (0,))
BOTH_FIRST = ((0,), (0,))


def kernel(
    n_blk, n_split,
    u_hbm, h_hbm, item_hbm, conf_hbm, u_out, i_out,
    users, users_hi, users_lo, slab_16, err_16, counts, grad, item_in, conf_in,
    held, outgoing, share_buf,
    load_sem, turn_sem, obs_send, obs_recv, u_send, u_recv, h_send, h_recv, share_send, share_recv,
):
    u_dev, rank = u_hbm.shape
    slab_rows = h_hbm.shape[0]
    share_rows = slab_rows // n_split
    piece = u_dev // PIECES
    col = rank // COLS
    blk = lax.axis_index("blk")
    spl = lax.axis_index("split")
    ahead = lax.rem(blk + n_blk - 1, n_blk)
    behind = lax.rem(blk + 1, n_blk)
    peers = [lax.rem(spl + q, n_split) for q in range(n_split)]
    share_at = pl.multiple_of(spl * share_rows, share_rows)

    barrier = pltpu.get_barrier_semaphore()
    for q in range(1, n_split):
        pl.semaphore_signal(barrier, inc=1, device_id=(blk, peers[q]), device_id_type=MESH)
    for other in (ahead, behind):
        pl.semaphore_signal(barrier, inc=1, device_id=(other, spl), device_id_type=MESH)
    loads = [
        pltpu.make_async_copy(there, here, load_sem.at[i])
        for i, (there, here) in enumerate((
            (u_hbm, users.at[pl.ds(0, u_dev)]),
            (item_hbm, item_in.at[0]),
            (conf_hbm, conf_in.at[0]),
            *((h_hbm.at[:, pl.ds(c * col, col)], held.at[0, c]) for c in range(COLS)),
        ))
    ]
    for load in loads:
        load.start()
    pl.semaphore_wait(barrier, n_split + 1)

    def obs_copies(q, part, steps):
        slot = n_split - q
        copies = []
        for i, (here, there) in enumerate(((item_hbm, item_in), (conf_hbm, conf_in))):
            copy = pltpu.make_async_remote_copy(
                src_ref=here.at[steps], dst_ref=there.at[slot, steps],
                send_sem=obs_send.at[q - 1, part, i], recv_sem=obs_recv.at[slot - 1, part, i],
                device_id=(blk, peers[q]), device_id_type=MESH,
            )
            copies.append(copy)
        return copies

    first, rest = pl.ds(0, 2), pl.ds(2, SUBS - 2)
    first_obs = [None] + [obs_copies(q, 0, first) for q in range(1, n_split)]
    rest_obs = [None] + [obs_copies(q, 1, rest) for q in range(1, n_split)]
    for copies in first_obs[1:]:
        for copy in copies:
            copy.start()
    user_copies = [None] + [
        [
            pltpu.make_async_remote_copy(
                src_ref=u_hbm.at[pl.ds(p * piece, piece)],
                dst_ref=users.at[pl.ds((n_split - q) * u_dev + p * piece, piece)],
                send_sem=u_send.at[q - 1, p], recv_sem=u_recv.at[n_split - q - 1, p],
                device_id=(blk, peers[q]), device_id_type=MESH,
            )
            for p in range(PIECES)
        ]
        for q in range(1, n_split)
    ]

    def send_users():
        for q in range(1, n_split):
            for copy in user_copies[q]:
                copy.start()

    paired = n_blk % 2 == 0
    even = lax.rem(blk, 2) == 0 if paired else blk >= 0
    pl.when(even)(send_users)

    def count(q, start, stop):
        rows = lax.broadcasted_iota(jnp.int32, (slab_rows, u_dev), 0)

        @pl.loop(start, stop)
        def _(step):
            total = jnp.zeros((slab_rows, u_dev), jnp.float32)
            for k in range(item_in.shape[2]):
                item = item_in[q, step, k:k + 1, :]
                conf = conf_in[q, step, k:k + 1, :].astype(jnp.float32)
                total = total + jnp.where(rows == item, conf, 0.0)
            counts[step, :, q * u_dev:(q + 1) * u_dev] = total

    def errors(scores, r):
        target = jnp.where(r > 0, 1.0, 0.0).astype(jnp.float32)
        return (1.0 + CONF_SCALE * r) * (scores - target)

    def split_users(rows):
        high, low = halves(users[rows, :])
        users_hi[rows, :] = high
        users_lo[rows, :] = low

    def split_slab(step, c):
        columns = columns_of[c]
        high, low = halves(held[step, c])
        slab_16[0:slab_rows, columns] = high
        slab_16[slab_rows:2 * slab_rows, columns] = low
        slab_16[2 * slab_rows:, columns] = high

    def scores_of(rows, columns):
        return stacked(
            slab_16[0:2 * slab_rows, columns],
            (users_hi[rows, columns], users_lo[rows, columns]),
            BOTH_LAST,
        )

    def keep_errors(step, rows, scores):
        high, low = halves(errors(scores, counts[step, :, rows]))
        err_16[0:slab_rows, rows] = high
        err_16[slab_rows:2 * slab_rows, rows] = high
        err_16[2 * slab_rows:, rows] = low

    def item_grad(rows, columns):
        return stacked(
            err_16[slab_rows:, rows], (users_hi[rows, columns], users_lo[rows, columns]), PLAIN
        )

    def user_step(rows):
        grad_user = dot(err_16[:, rows], slab_16[...], BOTH_FIRST)
        old = users[rows, :]
        return old - LEARN_RATE * (grad_user + RIDGE_COEF * old)

    def slab_copy(step, c):
        return pltpu.make_async_remote_copy(
            src_ref=outgoing.at[step, c], dst_ref=held.at[step + 1, c],
            send_sem=h_send.at[step, c], recv_sem=h_recv.at[step, c],
            device_id=(ahead, spl), device_id_type=MESH,
        )

    def send_slab(step, c, total):
        old = held[step, c]
        outgoing[step, c] = old - LEARN_RATE * (total + RIDGE_COEF * old)
        slab_copy(step, c).start()

    whole = slice(0, rank)
    every = slice(0, n_split * u_dev)
    own = slice(0, u_dev)
    columns_of = [slice(c * col, (c + 1) * col) for c in range(COLS)]

    for load in loads:
        load.wait()
    split_users(own)
    for c in range(COLS):
        split_slab(0, c)
    count(0, 0, SUBS)
    keep_errors(0, own, scores_of(own, whole))
    grad[...] = item_grad(own, whole)
    for q in range(1, n_split):
        for copy in first_obs[n_split - q]:
            copy.wait_recv()
        count(q, 0, 2)
    if paired:

        @pl.when(jnp.logical_not(even))
        def _():
            pl.semaphore_wait(turn_sem, 1)
            send_users()

    part = u_dev // PARTS
    for q in range(1, n_split):
        for p in range(PIECES):
            user_copies[n_split - q][p].wait_recv()
            if paired and q == n_split - 1 and p == PIECES - 2:

                @pl.when(even)
                def _():
                    pl.semaphore_signal(
                        turn_sem, inc=1, device_id=(behind, spl), device_id_type=MESH
                    )

            done = (p + 1) * piece
            if done % part == 0:
                rows = slice(q * u_dev + done - part, q * u_dev + done)
                split_users(rows)
                keep_errors(0, rows, scores_of(rows, whole))
                if q < n_split - 1 or p < PIECES - 1:
                    grad[...] += item_grad(rows, whole)
    for c, columns in enumerate(columns_of):
        send_slab(0, c, grad[:, columns] + item_grad(rows, columns))

    def update_users():
        @pl.loop(0, n_split)
        def _(q):
            rows = pl.ds(pl.multiple_of(q * u_dev, u_dev), u_dev)
            users[rows, :] = user_step(rows)
            split_users(rows)

    update_users()

    @pl.loop(1, SUBS - 1)
    def _(step):
        scores = 0.0
        for c, columns in enumerate(columns_of):
            slab_copy(step - 1, c).wait_recv()
            split_slab(step, c)
            scores = scores + scores_of(every, columns)
        keep_errors(step, every, scores)

        @pl.when(step == 1)
        def _():
            for copies in rest_obs[1:]:
                for copy in copies:
                    copy.start()

        for c, columns in enumerate(columns_of):
            send_slab(step, c, item_grad(every, columns))
        update_users()

        @pl.when(step == 1)
        def _():
            for q in range(1, n_split):
                for copy in rest_obs[n_split - q]:
                    copy.wait_recv()
                count(q, 2, SUBS)

    last = SUBS - 1
    share = pl.ds(share_at, share_rows)
    low_share = pl.ds(pl.multiple_of(slab_rows + share_at, share_rows), share_rows)
    scores = 0.0
    for c, columns in enumerate(columns_of):
        slab_copy(last - 1, c).wait_recv()
        split_slab(last, c)
        scores = scores + stacked(
            jnp.concatenate([slab_16[share, columns], slab_16[low_share, columns]], axis=0),
            (users_hi[:, columns], users_lo[:, columns]),
            BOTH_LAST,
        )
    share_errors = jnp.concatenate(halves(errors(scores, counts[last, share, :])), axis=0)
    share_copies = []
    for c, columns in enumerate(columns_of):
        total = stacked(share_errors, (users_hi[:, columns], users_lo[:, columns]), PLAIN)
        old = held[last, c, share, :]
        share_buf[c] = old - LEARN_RATE * (total + RIDGE_COEF * old)
        copy = pltpu.make_async_remote_copy(
            src_ref=share_buf.at[c], dst_ref=i_out.at[:, pl.ds(c * col, col)],
            send_sem=share_send.at[c], recv_sem=share_recv.at[c],
            device_id=(ahead, spl), device_id_type=MESH,
        )
        copy.start()
        share_copies.append(copy)
    keep_errors(last, own, scores_of(own, whole))
    users[own, :] = user_step(own)
    store = pltpu.make_async_copy(users.at[pl.ds(0, u_dev)], u_out, load_sem.at[0])
    store.start()

    for q in range(1, n_split):
        for copy in first_obs[q] + rest_obs[q] + user_copies[q]:
            copy.wait_send()
    for step in range(last):
        for c in range(COLS):
            slab_copy(step, c).wait_send()
    for copy in share_copies:
        copy.wait_send()
        copy.wait_recv()
    store.wait()


def store_kernel(u_in, i_in, u_out, i_out, u_buf, i_buf, load_sem, store_sem):
    rows = u_in.shape[0] // PIECES
    pieces = [(i_in, i_buf, i_out)]
    for p in range(PIECES):
        at = pl.ds(p * rows, rows)
        pieces.append((u_in.at[at], u_buf.at[at], u_out.at[at]))
    loads = [
        pltpu.make_async_copy(there, here, load_sem.at[i]) for i, (there, here, _) in enumerate(pieces)
    ]
    stores = [
        pltpu.make_async_copy(here, out, store_sem.at[i]) for i, (_, here, out) in enumerate(pieces)
    ]
    for load in loads:
        load.start()
    for load, store in zip(loads, stores):
        load.wait()
        store.start()
    for store in stores:
        store.wait()


def local(n_blk, n_split, user_factors, item_factors, obs_items, obs_conf):
    u_dev, rank = user_factors.shape
    slab_rows = item_factors.shape[0]
    share_rows = slab_rows // n_split
    subs = obs_items.shape[1]
    items, confs = (obs.transpose(1, 2, 0) for obs in (obs_items, obs_conf))
    everyone = n_split * u_dev
    f32, b16 = jnp.float32, jnp.bfloat16
    dma = pltpu.SemaphoreType.DMA
    results = pl.pallas_call(
        functools.partial(kernel, n_blk, n_split),
        out_shape=(
            jax.ShapeDtypeStruct((u_dev, rank), f32),
            jax.ShapeDtypeStruct((share_rows, rank), f32),
        ),
        in_specs=[pl.BlockSpec(memory_space=pltpu.HBM)] * 4,
        out_specs=(pl.BlockSpec(memory_space=pl.ANY),) * 2,
        scratch_shapes=[
            pltpu.VMEM((everyone, rank), f32),
            pltpu.VMEM((everyone, rank), b16),
            pltpu.VMEM((everyone, rank), b16),
            pltpu.VMEM((3 * slab_rows, rank), b16),
            pltpu.VMEM((3 * slab_rows, everyone), b16),
            pltpu.VMEM((subs, slab_rows, everyone), f32),
            pltpu.VMEM((slab_rows, rank), f32),
            pltpu.VMEM((n_split,) + items.shape, jnp.int32),
            pltpu.VMEM((n_split,) + items.shape, jnp.int32),
            pltpu.VMEM((subs, COLS, slab_rows, rank // COLS), f32),
            pltpu.VMEM((subs - 1, COLS, slab_rows, rank // COLS), f32),
            pltpu.VMEM((COLS, share_rows, rank // COLS), f32),
            dma((3 + COLS,)),
            pltpu.SemaphoreType.REGULAR,
            dma((n_split - 1, 2, 2)),
            dma((n_split - 1, 2, 2)),
            dma((n_split - 1, PIECES)),
            dma((n_split - 1, PIECES)),
            dma((subs - 1, COLS)),
            dma((subs - 1, COLS)),
            dma((COLS,)),
            dma((COLS,)),
        ],
        compiler_params=pltpu.CompilerParams(
            collective_id=0, has_side_effects=True, vmem_limit_bytes=63 * 2**20
        ),
    )(user_factors, item_factors, items, confs)
    return pl.pallas_call(
        store_kernel,
        out_shape=tuple(jax.ShapeDtypeStruct(x.shape, x.dtype) for x in results),
        in_specs=[pl.BlockSpec(memory_space=pl.ANY)] * 2,
        out_specs=(pl.BlockSpec(memory_space=pl.ANY),) * 2,
        scratch_shapes=[
            *(pltpu.VMEM(x.shape, x.dtype) for x in results),
            dma((PIECES + 1,)),
            dma((PIECES + 1,)),
        ],
        compiler_params=pltpu.CompilerParams(vmem_limit_bytes=63 * 2**20),
    )(*results)


def solution(mesh):
    in_specs = (
        P(("blk", "split"), None),
        P("blk", None),
        P(("blk", "split"), None, None),
        P(("blk", "split"), None, None),
    )
    out_specs = (P(("blk", "split"), None), P(("blk", "split"), None))
    body = functools.partial(local, mesh.shape["blk"], mesh.shape["split"])
    return jax.shard_map(body, mesh=mesh, in_specs=in_specs, out_specs=out_specs, check_vma=False)
```

```python
import functools

import jax
import jax.numpy as jnp
from jax import lax
from jax.experimental import pallas as pl
from jax.experimental.pallas import tpu as pltpu
from jax.sharding import PartitionSpec as P

SUBS = 4


LEARN_RATE = 0.0005
CONF_SCALE = 0.5
RIDGE_COEF = 0.01

MESH = pl.DeviceIdType.MESH
PIECES = 4
PARTS = 2
COLS = 2


def halves(x):
    high = x.astype(jnp.bfloat16)
    return high, (x - high.astype(jnp.float32)).astype(jnp.bfloat16)


def dot(a, b, dims):
    return lax.dot_general(a, b, (dims, ((), ())), preferred_element_type=jnp.float32)


def stacked(a, b, dims):
    rows = a.shape[0] // 2
    both = dot(a, b[0], dims)
    return both[:rows] + (both[rows:] + dot(a[:rows], b[1], dims))


BOTH_LAST = ((1,), (1,))
PLAIN = ((1,), (0,))
BOTH_FIRST = ((0,), (0,))


def kernel(
    n_blk, n_split,
    u_hbm, h_hbm, item_hbm, conf_hbm, u_out, i_out,
    users, users_hi, users_lo, slab_16, err_16, counts, grad, item_in, conf_in,
    held, outgoing,
    load_sem, obs_send, obs_recv, u_send, u_recv, h_send, h_recv, share_send, share_recv,
):
    u_dev, rank = u_hbm.shape
    slab_rows = h_hbm.shape[0]
    share_rows = slab_rows // n_split
    piece = u_dev // PIECES
    col = rank // COLS
    blk = lax.axis_index("blk")
    spl = lax.axis_index("split")
    ahead = lax.rem(blk + n_blk - 1, n_blk)
    behind = lax.rem(blk + 1, n_blk)
    main = lax.rem(blk, n_split)
    is_main = spl == main
    is_side = jnp.logical_not(is_main)
    peers = [lax.rem(spl + q, n_split) for q in range(n_split)]
    takers = [lax.rem(lax.rem(ahead, n_split) + q, n_split) for q in range(n_split)]

    barrier = pltpu.get_barrier_semaphore()
    pl.semaphore_signal(
        barrier, inc=1, device_id=(behind, lax.rem(behind, n_split)), device_id_type=MESH
    )

    @pl.when(is_main)
    def _():
        for q in range(1, n_split):
            pl.semaphore_signal(barrier, inc=1, device_id=(blk, peers[q]), device_id_type=MESH)

    loads = [
        pltpu.make_async_copy(there, here, load_sem.at[i])
        for i, (there, here) in enumerate((
            (u_hbm, users.at[pl.ds(0, u_dev)]),
            (item_hbm, item_in.at[0]),
            (conf_hbm, conf_in.at[0]),
            *((h_hbm.at[:, pl.ds(c * col, col)], held.at[0, c]) for c in range(COLS)),
        ))
    ]
    for load in loads:
        load.start()
    first, rest = pl.ds(0, 2), pl.ds(2, SUBS - 2)

    def obs_copies(slot, part):
        steps = (first, rest)[part]
        return [
            pltpu.make_async_remote_copy(
                src_ref=here.at[steps], dst_ref=there.at[slot, steps],
                send_sem=obs_send.at[part, i], recv_sem=obs_recv.at[slot - 1, part, i],
                device_id=(blk, main), device_id_type=MESH,
            )
            for i, (here, there) in enumerate(((item_hbm, item_in), (conf_hbm, conf_in)))
        ]

    def user_copy(slot, p):
        at = pl.multiple_of(slot * u_dev + p * piece, piece)
        return pltpu.make_async_remote_copy(
            src_ref=u_hbm.at[pl.ds(p * piece, piece)], dst_ref=users.at[pl.ds(at, piece)],
            send_sem=u_send.at[p], recv_sem=u_recv.at[slot - 1, p],
            device_id=(blk, main), device_id_type=MESH,
        )

    my_slot = lax.rem(spl - main + n_split, n_split)

    @pl.when(is_side)
    def _():
        pl.semaphore_wait(barrier, 1)
        for copy in obs_copies(my_slot, 0):
            copy.start()
        for p in range(PIECES):
            user_copy(my_slot, p).start()

    def count(q, start, stop):
        rows = lax.broadcasted_iota(jnp.int32, (slab_rows, u_dev), 0)

        @pl.loop(start, stop)
        def _(step):
            total = jnp.zeros((slab_rows, u_dev), jnp.float32)
            for k in range(item_in.shape[2]):
                item = item_in[q, step, k:k + 1, :]
                conf = conf_in[q, step, k:k + 1, :].astype(jnp.float32)
                total = total + jnp.where(rows == item, conf, 0.0)
            counts[step, :, q * u_dev:(q + 1) * u_dev] = total

    def errors(scores, r):
        target = jnp.where(r > 0, 1.0, 0.0).astype(jnp.float32)
        return (1.0 + CONF_SCALE * r) * (scores - target)

    def split_users(rows):
        high, low = halves(users[rows, :])
        users_hi[rows, :] = high
        users_lo[rows, :] = low

    def split_slab(step, c):
        columns = columns_of[c]
        high, low = halves(held[step, c])
        slab_16[0:slab_rows, columns] = high
        slab_16[slab_rows:2 * slab_rows, columns] = low
        slab_16[2 * slab_rows:, columns] = high

    def scores_of(rows, columns):
        return stacked(
            slab_16[0:2 * slab_rows, columns],
            (users_hi[rows, columns], users_lo[rows, columns]),
            BOTH_LAST,
        )

    def keep_errors(step, rows, scores):
        high, low = halves(errors(scores, counts[step, :, rows]))
        err_16[0:slab_rows, rows] = high
        err_16[slab_rows:2 * slab_rows, rows] = high
        err_16[2 * slab_rows:, rows] = low

    def item_grad(rows, columns):
        return stacked(
            err_16[slab_rows:, rows], (users_hi[rows, columns], users_lo[rows, columns]), PLAIN
        )

    def user_step(rows):
        grad_user = dot(err_16[:, rows], slab_16[...], BOTH_FIRST)
        old = users[rows, :]
        return old - LEARN_RATE * (grad_user + RIDGE_COEF * old)

    def slab_copy(step, c, q):
        return pltpu.make_async_remote_copy(
            src_ref=outgoing.at[step, c], dst_ref=held.at[step + 1, c],
            send_sem=h_send.at[step, c, q], recv_sem=h_recv.at[step, c],
            device_id=(ahead, takers[q]), device_id_type=MESH,
        )

    def share_copy(c, q):
        at = pl.multiple_of(takers[q] * share_rows, share_rows)
        return pltpu.make_async_remote_copy(
            src_ref=outgoing.at[SUBS - 1, c, pl.ds(at, share_rows)],
            dst_ref=i_out.at[:, pl.ds(c * col, col)],
            send_sem=share_send.at[c, q], recv_sem=share_recv.at[c],
            device_id=(ahead, takers[q]), device_id_type=MESH,
        )

    def pass_on(step, copy_of, grad_of):
        for c, columns in enumerate(columns_of):
            old = held[step, c]
            outgoing[step, c] = old - LEARN_RATE * (grad_of(columns) + RIDGE_COEF * old)
            copy_of(c, 0).start()
        for q in range(1, n_split):
            for c in range(COLS):
                copy_of(c, q).start()

    whole = slice(0, rank)
    every = slice(0, n_split * u_dev)
    own = slice(0, u_dev)
    columns_of = [slice(c * col, (c + 1) * col) for c in range(COLS)]

    for load in loads:
        load.wait()
    split_users(own)
    for c in range(COLS):
        split_slab(0, c)
    count(0, 0, SUBS)
    keep_errors(0, own, scores_of(own, whole))
    last = SUBS - 1
    part = u_dev // PARTS

    def update(groups):
        @pl.loop(0, groups)
        def _(q):
            rows = pl.ds(pl.multiple_of(q * u_dev, u_dev), u_dev)
            users[rows, :] = user_step(rows)
            split_users(rows)

    def meet_slab(step, rows):
        scores = 0.0
        for c, columns in enumerate(columns_of):
            slab_copy(step - 1, c, 0).wait_recv()
            split_slab(step, c)
            scores = scores + scores_of(rows, columns)
        keep_errors(step, rows, scores)

    @pl.when(is_main)
    def _():
        grad[...] = item_grad(own, whole)
        pl.semaphore_wait(barrier, n_split)
        for q in range(1, n_split):
            for copy in obs_copies(q, 0):
                copy.wait_recv()
            count(q, 0, 2)
        for q in range(1, n_split):
            for p in range(PIECES):
                user_copy(q, p).wait_recv()
                done = (p + 1) * piece
                if done % part == 0:
                    rows = slice(q * u_dev + done - part, q * u_dev + done)
                    split_users(rows)
                    keep_errors(0, rows, scores_of(rows, whole))
                    if q < n_split - 1 or p < PIECES - 1:
                        grad[...] += item_grad(rows, whole)
        pass_on(
            0,
            functools.partial(slab_copy, 0),
            lambda columns: grad[:, columns] + item_grad(rows, columns),
        )
        update(n_split)
        for q in range(1, n_split):
            for copy in obs_copies(q, 1):
                copy.wait_recv()
            count(q, 2, SUBS)

        @pl.loop(1, last)
        def _(step):
            meet_slab(step, every)
            pass_on(step, functools.partial(slab_copy, step), functools.partial(item_grad, every))
            update(n_split)

        meet_slab(last, every)
        pass_on(last, share_copy, functools.partial(item_grad, every))

    @pl.when(is_side)
    def _():
        update(1)
        for p in range(PIECES):
            user_copy(my_slot, p).wait_send()
        for copy in obs_copies(my_slot, 1):
            copy.start()

        @pl.loop(1, last)
        def _(step):
            meet_slab(step, own)
            update(1)

        meet_slab(last, own)

    users[own, :] = user_step(own)
    store = pltpu.make_async_copy(users.at[pl.ds(0, u_dev)], u_out, load_sem.at[0])
    store.start()

    @pl.when(is_main)
    def _():
        for q in range(n_split):
            for c in range(COLS):
                for step in range(last):
                    slab_copy(step, c, q).wait_send()
                share_copy(c, q).wait_send()

    @pl.when(is_side)
    def _():
        for copy in obs_copies(my_slot, 0) + obs_copies(my_slot, 1):
            copy.wait_send()

    for c in range(COLS):
        share_copy(c, 0).wait_recv()
    store.wait()


def store_kernel(u_in, i_in, u_out, i_out, u_buf, i_buf, load_sem, store_sem):
    rows = u_in.shape[0] // PIECES
    pieces = [(i_in, i_buf, i_out)]
    for p in range(PIECES):
        at = pl.ds(p * rows, rows)
        pieces.append((u_in.at[at], u_buf.at[at], u_out.at[at]))
    loads = [
        pltpu.make_async_copy(there, here, load_sem.at[i]) for i, (there, here, _) in enumerate(pieces)
    ]
    stores = [
        pltpu.make_async_copy(here, out, store_sem.at[i]) for i, (_, here, out) in enumerate(pieces)
    ]
    for load in loads:
        load.start()
    for load, store in zip(loads, stores):
        load.wait()
        store.start()
    for store in stores:
        store.wait()


def local(n_blk, n_split, user_factors, item_factors, obs_items, obs_conf):
    u_dev, rank = user_factors.shape
    slab_rows = item_factors.shape[0]
    share_rows = slab_rows // n_split
    subs = obs_items.shape[1]
    items, confs = (obs.transpose(1, 2, 0) for obs in (obs_items, obs_conf))
    everyone = n_split * u_dev
    f32, b16 = jnp.float32, jnp.bfloat16
    dma = pltpu.SemaphoreType.DMA
    results = pl.pallas_call(
        functools.partial(kernel, n_blk, n_split),
        out_shape=(
            jax.ShapeDtypeStruct((u_dev, rank), f32),
            jax.ShapeDtypeStruct((share_rows, rank), f32),
        ),
        in_specs=[pl.BlockSpec(memory_space=pltpu.HBM)] * 4,
        out_specs=(pl.BlockSpec(memory_space=pl.ANY),) * 2,
        scratch_shapes=[
            pltpu.VMEM((everyone, rank), f32),
            pltpu.VMEM((everyone, rank), b16),
            pltpu.VMEM((everyone, rank), b16),
            pltpu.VMEM((3 * slab_rows, rank), b16),
            pltpu.VMEM((3 * slab_rows, everyone), b16),
            pltpu.VMEM((subs, slab_rows, everyone), f32),
            pltpu.VMEM((slab_rows, rank), f32),
            pltpu.VMEM((n_split,) + items.shape, jnp.int32),
            pltpu.VMEM((n_split,) + items.shape, jnp.int32),
            pltpu.VMEM((subs, COLS, slab_rows, rank // COLS), f32),
            pltpu.VMEM((subs, COLS, slab_rows, rank // COLS), f32),
            dma((3 + COLS,)),
            dma((2, 2)),
            dma((n_split - 1, 2, 2)),
            dma((PIECES,)),
            dma((n_split - 1, PIECES)),
            dma((subs - 1, COLS, n_split)),
            dma((subs - 1, COLS)),
            dma((COLS, n_split)),
            dma((COLS,)),
        ],
        compiler_params=pltpu.CompilerParams(
            collective_id=0, has_side_effects=True, vmem_limit_bytes=63 * 2**20
        ),
    )(user_factors, item_factors, items, confs)
    return pl.pallas_call(
        store_kernel,
        out_shape=tuple(jax.ShapeDtypeStruct(x.shape, x.dtype) for x in results),
        in_specs=[pl.BlockSpec(memory_space=pl.ANY)] * 2,
        out_specs=(pl.BlockSpec(memory_space=pl.ANY),) * 2,
        scratch_shapes=[
            *(pltpu.VMEM(x.shape, x.dtype) for x in results),
            dma((PIECES + 1,)),
            dma((PIECES + 1,)),
        ],
        compiler_params=pltpu.CompilerParams(vmem_limit_bytes=63 * 2**20),
    )(*results)


def solution(mesh):
    in_specs = (
        P(("blk", "split"), None),
        P("blk", None),
        P(("blk", "split"), None, None),
        P(("blk", "split"), None, None),
    )
    out_specs = (P(("blk", "split"), None), P(("blk", "split"), None))
    body = functools.partial(local, mesh.shape["blk"], mesh.shape["split"])
    return jax.shard_map(body, mesh=mesh, in_specs=in_specs, out_specs=out_specs, check_vma=False)
```

```python
import functools

import jax
import jax.numpy as jnp
from jax import lax
from jax.experimental import pallas as pl
from jax.experimental.pallas import tpu as pltpu
from jax.sharding import PartitionSpec as P

SUBS = 4


LEARN_RATE = 0.0005
CONF_SCALE = 0.5
RIDGE_COEF = 0.01

MESH = pl.DeviceIdType.MESH
PIECES = 4
PARTS = 2
COLS = 2


def halves(x):
    high = x.astype(jnp.bfloat16)
    return high, (x - high.astype(jnp.float32)).astype(jnp.bfloat16)


def dot(a, b, dims):
    return lax.dot_general(a, b, (dims, ((), ())), preferred_element_type=jnp.float32)


def stacked(a, b, dims):
    rows = a.shape[0] // 2
    both = dot(a, b[0], dims)
    return both[:rows] + (both[rows:] + dot(a[:rows], b[1], dims))


BOTH_LAST = ((1,), (1,))
PLAIN = ((1,), (0,))
BOTH_FIRST = ((0,), (0,))


def kernel(
    n_blk, n_split,
    u_hbm, h_hbm, item_hbm, conf_hbm, u_out, i_out,
    users, users_hi, users_lo, slab_16, err_16, counts, grad, item_in, conf_in,
    held, outgoing,
    load_sem, obs_send, obs_recv, u_send, u_recv, h_send, h_recv, share_send, share_recv,
):
    u_dev, rank = u_hbm.shape
    slab_rows = h_hbm.shape[0]
    share_rows = slab_rows // n_split
    piece = u_dev // PIECES
    col = rank // COLS
    blk = lax.axis_index("blk")
    spl = lax.axis_index("split")
    ahead = lax.rem(blk + n_blk - 1, n_blk)
    behind = lax.rem(blk + 1, n_blk)
    def main_of(b):
        return lax.rem((b + 1) // 2, n_split)

    main = main_of(blk)
    is_main = spl == main
    is_side = jnp.logical_not(is_main)
    peers = [lax.rem(spl + q, n_split) for q in range(n_split)]
    takers = [lax.rem(main_of(ahead) + q, n_split) for q in range(n_split)]

    barrier = pltpu.get_barrier_semaphore()
    pl.semaphore_signal(barrier, inc=1, device_id=(behind, main_of(behind)), device_id_type=MESH)

    @pl.when(is_main)
    def _():
        for q in range(1, n_split):
            pl.semaphore_signal(barrier, inc=1, device_id=(blk, peers[q]), device_id_type=MESH)

    loads = [
        pltpu.make_async_copy(there, here, load_sem.at[i])
        for i, (there, here) in enumerate((
            (u_hbm, users.at[pl.ds(0, u_dev)]),
            (item_hbm, item_in.at[0]),
            (conf_hbm, conf_in.at[0]),
            *((h_hbm.at[:, pl.ds(c * col, col)], held.at[0, c]) for c in range(COLS)),
        ))
    ]
    for load in loads:
        load.start()
    first, rest = pl.ds(0, 2), pl.ds(2, SUBS - 2)

    def obs_copies(slot, part):
        steps = (first, rest)[part]
        return [
            pltpu.make_async_remote_copy(
                src_ref=here.at[steps], dst_ref=there.at[slot, steps],
                send_sem=obs_send.at[part, i], recv_sem=obs_recv.at[slot - 1, part, i],
                device_id=(blk, main), device_id_type=MESH,
            )
            for i, (here, there) in enumerate(((item_hbm, item_in), (conf_hbm, conf_in)))
        ]

    def user_copy(slot, p):
        at = pl.multiple_of(slot * u_dev + p * piece, piece)
        return pltpu.make_async_remote_copy(
            src_ref=u_hbm.at[pl.ds(p * piece, piece)], dst_ref=users.at[pl.ds(at, piece)],
            send_sem=u_send.at[p], recv_sem=u_recv.at[slot - 1, p],
            device_id=(blk, main), device_id_type=MESH,
        )

    my_slot = lax.rem(spl - main + n_split, n_split)

    @pl.when(is_side)
    def _():
        pl.semaphore_wait(barrier, 1)
        for copy in obs_copies(my_slot, 0):
            copy.start()
        for p in range(PIECES):
            user_copy(my_slot, p).start()

    def count(q, start, stop):
        rows = lax.broadcasted_iota(jnp.int32, (slab_rows, u_dev), 0)

        @pl.loop(start, stop)
        def _(step):
            total = jnp.zeros((slab_rows, u_dev), jnp.float32)
            for k in range(item_in.shape[2]):
                item = item_in[q, step, k:k + 1, :]
                conf = conf_in[q, step, k:k + 1, :].astype(jnp.float32)
                total = total + jnp.where(rows == item, conf, 0.0)
            counts[step, :, q * u_dev:(q + 1) * u_dev] = total

    def errors(scores, r):
        target = jnp.where(r > 0, 1.0, 0.0).astype(jnp.float32)
        return (1.0 + CONF_SCALE * r) * (scores - target)

    def split_users(rows):
        high, low = halves(users[rows, :])
        users_hi[rows, :] = high
        users_lo[rows, :] = low

    def split_slab(step, c):
        columns = columns_of[c]
        high, low = halves(held[step, c])
        slab_16[0:slab_rows, columns] = high
        slab_16[slab_rows:2 * slab_rows, columns] = low
        slab_16[2 * slab_rows:, columns] = high

    def scores_of(rows, columns):
        return stacked(
            slab_16[0:2 * slab_rows, columns],
            (users_hi[rows, columns], users_lo[rows, columns]),
            BOTH_LAST,
        )

    def keep_errors(step, rows, scores):
        high, low = halves(errors(scores, counts[step, :, rows]))
        err_16[0:slab_rows, rows] = high
        err_16[slab_rows:2 * slab_rows, rows] = high
        err_16[2 * slab_rows:, rows] = low

    def item_grad(rows, columns):
        return stacked(
            err_16[slab_rows:, rows], (users_hi[rows, columns], users_lo[rows, columns]), PLAIN
        )

    def user_step(rows):
        grad_user = dot(err_16[:, rows], slab_16[...], BOTH_FIRST)
        old = users[rows, :]
        return old - LEARN_RATE * (grad_user + RIDGE_COEF * old)

    def slab_copy(step, c, q):
        return pltpu.make_async_remote_copy(
            src_ref=outgoing.at[step, c], dst_ref=held.at[step + 1, c],
            send_sem=h_send.at[step, c, q], recv_sem=h_recv.at[step, c],
            device_id=(ahead, takers[q]), device_id_type=MESH,
        )

    def share_copy(c, q):
        at = pl.multiple_of(takers[q] * share_rows, share_rows)
        return pltpu.make_async_remote_copy(
            src_ref=outgoing.at[SUBS - 1, c, pl.ds(at, share_rows)],
            dst_ref=i_out.at[:, pl.ds(c * col, col)],
            send_sem=share_send.at[c, q], recv_sem=share_recv.at[c],
            device_id=(ahead, takers[q]), device_id_type=MESH,
        )

    def pass_on(step, copy_of, grad_of):
        for c, columns in enumerate(columns_of):
            old = held[step, c]
            outgoing[step, c] = old - LEARN_RATE * (grad_of(columns) + RIDGE_COEF * old)
            copy_of(c, 0).start()

    def pass_to_sides(copy_of):
        for c in range(COLS):
            copy_of(c, 0).wait_send()
        for q in range(1, n_split):
            for c in range(COLS):
                copy_of(c, q).start()

    whole = slice(0, rank)
    every = slice(0, n_split * u_dev)
    own = slice(0, u_dev)
    columns_of = [slice(c * col, (c + 1) * col) for c in range(COLS)]

    for load in loads:
        load.wait()
    split_users(own)
    for c in range(COLS):
        split_slab(0, c)
    count(0, 0, SUBS)
    keep_errors(0, own, scores_of(own, whole))
    last = SUBS - 1
    part = u_dev // PARTS

    def update(groups):
        @pl.loop(0, groups)
        def _(q):
            rows = pl.ds(pl.multiple_of(q * u_dev, u_dev), u_dev)
            users[rows, :] = user_step(rows)
            split_users(rows)

    def meet_slab(step, rows):
        scores = 0.0
        for c, columns in enumerate(columns_of):
            slab_copy(step - 1, c, 0).wait_recv()
            split_slab(step, c)
            scores = scores + scores_of(rows, columns)
        keep_errors(step, rows, scores)

    @pl.when(is_main)
    def _():
        grad[...] = item_grad(own, whole)
        pl.semaphore_wait(barrier, n_split)
        for q in range(1, n_split):
            for copy in obs_copies(q, 0):
                copy.wait_recv()
            count(q, 0, 2)
        for q in range(1, n_split):
            for p in range(PIECES):
                user_copy(q, p).wait_recv()
                done = (p + 1) * piece
                if done % part == 0:
                    rows = slice(q * u_dev + done - part, q * u_dev + done)
                    split_users(rows)
                    keep_errors(0, rows, scores_of(rows, whole))
                    if q < n_split - 1 or p < PIECES - 1:
                        grad[...] += item_grad(rows, whole)
        pass_on(
            0,
            functools.partial(slab_copy, 0),
            lambda columns: grad[:, columns] + item_grad(rows, columns),
        )
        update(n_split)
        pass_to_sides(functools.partial(slab_copy, 0))
        for q in range(1, n_split):
            for copy in obs_copies(q, 1):
                copy.wait_recv()
            count(q, 2, SUBS)

        @pl.loop(1, last)
        def _(step):
            meet_slab(step, every)
            pass_on(step, functools.partial(slab_copy, step), functools.partial(item_grad, every))
            update(n_split)
            pass_to_sides(functools.partial(slab_copy, step))

        meet_slab(last, every)
        pass_on(last, share_copy, functools.partial(item_grad, every))
        for q in range(1, n_split):
            for c in range(COLS):
                share_copy(c, q).start()

    @pl.when(is_side)
    def _():
        update(1)
        for p in range(PIECES):
            user_copy(my_slot, p).wait_send()
        for copy in obs_copies(my_slot, 1):
            copy.start()

        @pl.loop(1, last)
        def _(step):
            meet_slab(step, own)
            update(1)

        meet_slab(last, own)

    users[own, :] = user_step(own)
    store = pltpu.make_async_copy(users.at[pl.ds(0, u_dev)], u_out, load_sem.at[0])
    store.start()

    @pl.when(is_main)
    def _():
        for c in range(COLS):
            for q in range(1, n_split):
                for step in range(last):
                    slab_copy(step, c, q).wait_send()
            for q in range(n_split):
                share_copy(c, q).wait_send()

    @pl.when(is_side)
    def _():
        for copy in obs_copies(my_slot, 0) + obs_copies(my_slot, 1):
            copy.wait_send()

    for c in range(COLS):
        share_copy(c, 0).wait_recv()
    store.wait()


def store_kernel(u_in, i_in, u_out, i_out, u_buf, i_buf, load_sem, store_sem):
    rows = u_in.shape[0] // PIECES
    pieces = [(i_in, i_buf, i_out)]
    for p in range(PIECES):
        at = pl.ds(p * rows, rows)
        pieces.append((u_in.at[at], u_buf.at[at], u_out.at[at]))
    loads = [
        pltpu.make_async_copy(there, here, load_sem.at[i]) for i, (there, here, _) in enumerate(pieces)
    ]
    stores = [
        pltpu.make_async_copy(here, out, store_sem.at[i]) for i, (_, here, out) in enumerate(pieces)
    ]
    for load in loads:
        load.start()
    for load, store in zip(loads, stores):
        load.wait()
        store.start()
    for store in stores:
        store.wait()


def local(n_blk, n_split, user_factors, item_factors, obs_items, obs_conf):
    u_dev, rank = user_factors.shape
    slab_rows = item_factors.shape[0]
    share_rows = slab_rows // n_split
    subs = obs_items.shape[1]
    items, confs = (obs.transpose(1, 2, 0) for obs in (obs_items, obs_conf))
    everyone = n_split * u_dev
    f32, b16 = jnp.float32, jnp.bfloat16
    dma = pltpu.SemaphoreType.DMA
    results = pl.pallas_call(
        functools.partial(kernel, n_blk, n_split),
        out_shape=(
            jax.ShapeDtypeStruct((u_dev, rank), f32),
            jax.ShapeDtypeStruct((share_rows, rank), f32),
        ),
        in_specs=[pl.BlockSpec(memory_space=pltpu.HBM)] * 4,
        out_specs=(pl.BlockSpec(memory_space=pl.ANY),) * 2,
        scratch_shapes=[
            pltpu.VMEM((everyone, rank), f32),
            pltpu.VMEM((everyone, rank), b16),
            pltpu.VMEM((everyone, rank), b16),
            pltpu.VMEM((3 * slab_rows, rank), b16),
            pltpu.VMEM((3 * slab_rows, everyone), b16),
            pltpu.VMEM((subs, slab_rows, everyone), f32),
            pltpu.VMEM((slab_rows, rank), f32),
            pltpu.VMEM((n_split,) + items.shape, jnp.int32),
            pltpu.VMEM((n_split,) + items.shape, jnp.int32),
            pltpu.VMEM((subs, COLS, slab_rows, rank // COLS), f32),
            pltpu.VMEM((subs, COLS, slab_rows, rank // COLS), f32),
            dma((3 + COLS,)),
            dma((2, 2)),
            dma((n_split - 1, 2, 2)),
            dma((PIECES,)),
            dma((n_split - 1, PIECES)),
            dma((subs - 1, COLS, n_split)),
            dma((subs - 1, COLS)),
            dma((COLS, n_split)),
            dma((COLS,)),
        ],
        compiler_params=pltpu.CompilerParams(
            collective_id=0, has_side_effects=True, vmem_limit_bytes=63 * 2**20
        ),
    )(user_factors, item_factors, items, confs)
    return pl.pallas_call(
        store_kernel,
        out_shape=tuple(jax.ShapeDtypeStruct(x.shape, x.dtype) for x in results),
        in_specs=[pl.BlockSpec(memory_space=pl.ANY)] * 2,
        out_specs=(pl.BlockSpec(memory_space=pl.ANY),) * 2,
        scratch_shapes=[
            *(pltpu.VMEM(x.shape, x.dtype) for x in results),
            dma((PIECES + 1,)),
            dma((PIECES + 1,)),
        ],
        compiler_params=pltpu.CompilerParams(vmem_limit_bytes=63 * 2**20),
    )(*results)


def solution(mesh):
    in_specs = (
        P(("blk", "split"), None),
        P("blk", None),
        P(("blk", "split"), None, None),
        P(("blk", "split"), None, None),
    )
    out_specs = (P(("blk", "split"), None), P(("blk", "split"), None))
    body = functools.partial(local, mesh.shape["blk"], mesh.shape["split"])
    return jax.shard_map(body, mesh=mesh, in_specs=in_specs, out_specs=out_specs, check_vma=False)
```

```python
import functools

import jax
import jax.numpy as jnp
from jax import lax
from jax.experimental import pallas as pl
from jax.experimental.pallas import tpu as pltpu
from jax.sharding import PartitionSpec as P

SUBS = 4


LEARN_RATE = 0.0005
CONF_SCALE = 0.5
RIDGE_COEF = 0.01

MESH = pl.DeviceIdType.MESH
PIECES = 4
PARTS = 2
COLS = 2


def halves(x):
    high = x.astype(jnp.bfloat16)
    return high, (x - high.astype(jnp.float32)).astype(jnp.bfloat16)


def dot(a, b, dims):
    return lax.dot_general(a, b, (dims, ((), ())), preferred_element_type=jnp.float32)


def stacked(a, b, dims):
    rows = a.shape[0] // 2
    both = dot(a, b[0], dims)
    return both[:rows] + (both[rows:] + dot(a[:rows], b[1], dims))


BOTH_LAST = ((1,), (1,))
PLAIN = ((1,), (0,))
BOTH_FIRST = ((0,), (0,))


def kernel(
    n_blk, n_split,
    u_hbm, h_hbm, item_hbm, conf_hbm, u_out, i_out,
    users, users_hi, users_lo, slab_16, err_16, counts, grad, item_in, conf_in,
    held, outgoing, share_buf,
    load_sem, turn_sem, obs_send, obs_recv, u_send, u_recv, h_send, h_recv, share_send, share_recv,
):
    u_dev, rank = u_hbm.shape
    slab_rows = h_hbm.shape[0]
    share_rows = slab_rows // n_split
    piece = u_dev // PIECES
    col = rank // COLS
    blk = lax.axis_index("blk")
    spl = lax.axis_index("split")
    ahead = lax.rem(blk + n_blk - 1, n_blk)
    behind = lax.rem(blk + 1, n_blk)
    peers = [lax.rem(spl + q, n_split) for q in range(n_split)]
    share_at = pl.multiple_of(spl * share_rows, share_rows)

    barrier = pltpu.get_barrier_semaphore()
    for q in range(1, n_split):
        pl.semaphore_signal(barrier, inc=1, device_id=(blk, peers[q]), device_id_type=MESH)
    for other in (ahead, behind):
        pl.semaphore_signal(barrier, inc=1, device_id=(other, spl), device_id_type=MESH)
    loads = [
        pltpu.make_async_copy(there, here, load_sem.at[i])
        for i, (there, here) in enumerate((
            (u_hbm, users.at[pl.ds(0, u_dev)]),
            (item_hbm, item_in.at[0]),
            (conf_hbm, conf_in.at[0]),
            *((h_hbm.at[:, pl.ds(c * col, col)], held.at[0, c]) for c in range(COLS)),
        ))
    ]
    for load in loads:
        load.start()
    pl.semaphore_wait(barrier, n_split + 1)

    def obs_copies(q, part, steps):
        slot = n_split - q
        copies = []
        for i, (here, there) in enumerate(((item_hbm, item_in), (conf_hbm, conf_in))):
            copy = pltpu.make_async_remote_copy(
                src_ref=here.at[steps], dst_ref=there.at[slot, steps],
                send_sem=obs_send.at[q - 1, part, i], recv_sem=obs_recv.at[slot - 1, part, i],
                device_id=(blk, peers[q]), device_id_type=MESH,
            )
            copies.append(copy)
        return copies

    first, rest = pl.ds(0, 2), pl.ds(2, SUBS - 2)
    first_obs = [None] + [obs_copies(q, 0, first) for q in range(1, n_split)]
    rest_obs = [None] + [obs_copies(q, 1, rest) for q in range(1, n_split)]
    for copies in first_obs[1:]:
        for copy in copies:
            copy.start()
    user_copies = [None] + [
        [
            pltpu.make_async_remote_copy(
                src_ref=u_hbm.at[pl.ds(p * piece, piece)],
                dst_ref=users.at[pl.ds((n_split - q) * u_dev + p * piece, piece)],
                send_sem=u_send.at[q - 1, p], recv_sem=u_recv.at[n_split - q - 1, p],
                device_id=(blk, peers[q]), device_id_type=MESH,
            )
            for p in range(PIECES)
        ]
        for q in range(1, n_split)
    ]

    def send_users():
        for q in range(1, n_split):
            for copy in user_copies[q]:
                copy.start()

    paired = n_blk % 2 == 0
    even = lax.rem(blk, 2) == 0 if paired else blk >= 0
    pl.when(even)(send_users)

    def count(q, start, stop):
        rows = lax.broadcasted_iota(jnp.int32, (slab_rows, u_dev), 0)

        @pl.loop(start, stop)
        def _(step):
            total = jnp.zeros((slab_rows, u_dev), jnp.float32)
            for k in range(item_in.shape[2]):
                item = item_in[q, step, k:k + 1, :]
                conf = conf_in[q, step, k:k + 1, :].astype(jnp.float32)
                total = total + jnp.where(rows == item, conf, 0.0)
            counts[step, :, q * u_dev:(q + 1) * u_dev] = total

    def errors(scores, r):
        target = jnp.where(r > 0, 1.0, 0.0).astype(jnp.float32)
        return (1.0 + CONF_SCALE * r) * (scores - target)

    def split_users(rows):
        high, low = halves(users[rows, :])
        users_hi[rows, :] = high
        users_lo[rows, :] = low

    def split_slab(step, c):
        columns = columns_of[c]
        high, low = halves(held[step, c])
        slab_16[0:slab_rows, columns] = high
        slab_16[slab_rows:2 * slab_rows, columns] = low
        slab_16[2 * slab_rows:, columns] = high

    def scores_of(rows, columns):
        return stacked(
            slab_16[0:2 * slab_rows, columns],
            (users_hi[rows, columns], users_lo[rows, columns]),
            BOTH_LAST,
        )

    def keep_errors(step, rows, scores):
        high, low = halves(errors(scores, counts[step, :, rows]))
        err_16[0:slab_rows, rows] = high
        err_16[slab_rows:2 * slab_rows, rows] = high
        err_16[2 * slab_rows:, rows] = low

    def item_grad(rows, columns):
        return stacked(
            err_16[slab_rows:, rows], (users_hi[rows, columns], users_lo[rows, columns]), PLAIN
        )

    def user_step(rows):
        grad_user = dot(err_16[:, rows], slab_16[...], BOTH_FIRST)
        old = users[rows, :]
        return old - LEARN_RATE * (grad_user + RIDGE_COEF * old)

    def slab_copy(step, c):
        return pltpu.make_async_remote_copy(
            src_ref=outgoing.at[step, c], dst_ref=held.at[step + 1, c],
            send_sem=h_send.at[step, c], recv_sem=h_recv.at[step, c],
            device_id=(ahead, spl), device_id_type=MESH,
        )

    def send_slab(step, c, total):
        old = held[step, c]
        outgoing[step, c] = old - LEARN_RATE * (total + RIDGE_COEF * old)
        slab_copy(step, c).start()

    whole = slice(0, rank)
    every = slice(0, n_split * u_dev)
    own = slice(0, u_dev)
    columns_of = [slice(c * col, (c + 1) * col) for c in range(COLS)]

    for load in loads:
        load.wait()
    split_users(own)
    for c in range(COLS):
        split_slab(0, c)
    count(0, 0, SUBS)
    keep_errors(0, own, scores_of(own, whole))
    grad[...] = item_grad(own, whole)
    for q in range(1, n_split):
        for copy in first_obs[n_split - q]:
            copy.wait_recv()
        count(q, 0, 2)
    if paired:

        @pl.when(jnp.logical_not(even))
        def _():
            pl.semaphore_wait(turn_sem, 1)
            send_users()

    part = u_dev // PARTS
    for q in range(1, n_split):
        for p in range(PIECES):
            user_copies[n_split - q][p].wait_recv()
            if paired and q == n_split - 1 and p == PIECES // 2 - 1:

                @pl.when(even)
                def _():
                    pl.semaphore_signal(
                        turn_sem, inc=1, device_id=(behind, spl), device_id_type=MESH
                    )

            done = (p + 1) * piece
            if done % part == 0:
                rows = slice(q * u_dev + done - part, q * u_dev + done)
                split_users(rows)
                keep_errors(0, rows, scores_of(rows, whole))
                if q < n_split - 1 or p < PIECES - 1:
                    grad[...] += item_grad(rows, whole)
    for c, columns in enumerate(columns_of):
        send_slab(0, c, grad[:, columns] + item_grad(rows, columns))

    def update_users():
        @pl.loop(0, n_split)
        def _(q):
            rows = pl.ds(pl.multiple_of(q * u_dev, u_dev), u_dev)
            users[rows, :] = user_step(rows)
            split_users(rows)

    update_users()

    @pl.loop(1, SUBS - 1)
    def _(step):
        scores = 0.0
        for c, columns in enumerate(columns_of):
            slab_copy(step - 1, c).wait_recv()
            split_slab(step, c)
            scores = scores + scores_of(every, columns)
        keep_errors(step, every, scores)

        @pl.when(step == 1)
        def _():
            for copies in rest_obs[1:]:
                for copy in copies:
                    copy.start()

        for c, columns in enumerate(columns_of):
            send_slab(step, c, item_grad(every, columns))
        update_users()

        @pl.when(step == 1)
        def _():
            for q in range(1, n_split):
                for copy in rest_obs[n_split - q]:
                    copy.wait_recv()
                count(q, 2, SUBS)

    last = SUBS - 1
    share = pl.ds(share_at, share_rows)
    low_share = pl.ds(pl.multiple_of(slab_rows + share_at, share_rows), share_rows)
    scores = 0.0
    for c, columns in enumerate(columns_of):
        slab_copy(last - 1, c).wait_recv()
        split_slab(last, c)
        scores = scores + stacked(
            jnp.concatenate([slab_16[share, columns], slab_16[low_share, columns]], axis=0),
            (users_hi[:, columns], users_lo[:, columns]),
            BOTH_LAST,
        )
    share_errors = jnp.concatenate(halves(errors(scores, counts[last, share, :])), axis=0)
    share_copies = []
    for c, columns in enumerate(columns_of):
        total = stacked(share_errors, (users_hi[:, columns], users_lo[:, columns]), PLAIN)
        old = held[last, c, share, :]
        share_buf[c] = old - LEARN_RATE * (total + RIDGE_COEF * old)
        copy = pltpu.make_async_remote_copy(
            src_ref=share_buf.at[c], dst_ref=i_out.at[:, pl.ds(c * col, col)],
            send_sem=share_send.at[c], recv_sem=share_recv.at[c],
            device_id=(ahead, spl), device_id_type=MESH,
        )
        copy.start()
        share_copies.append(copy)
    keep_errors(last, own, scores_of(own, whole))
    users[own, :] = user_step(own)
    store = pltpu.make_async_copy(users.at[pl.ds(0, u_dev)], u_out, load_sem.at[0])
    store.start()

    for q in range(1, n_split):
        for copy in first_obs[q] + rest_obs[q] + user_copies[q]:
            copy.wait_send()
    for step in range(last):
        for c in range(COLS):
            slab_copy(step, c).wait_send()
    for copy in share_copies:
        copy.wait_send()
        copy.wait_recv()
    store.wait()


def store_kernel(u_in, i_in, u_out, i_out, u_buf, i_buf, load_sem, store_sem):
    rows = u_in.shape[0] // PARTS
    pieces = [(i_in, i_buf, i_out)]
    for p in range(PARTS):
        at = pl.ds(p * rows, rows)
        pieces.append((u_in.at[at], u_buf.at[at], u_out.at[at]))
    loads = [
        pltpu.make_async_copy(there, here, load_sem.at[i]) for i, (there, here, _) in enumerate(pieces)
    ]
    stores = [
        pltpu.make_async_copy(here, out, store_sem.at[i]) for i, (_, here, out) in enumerate(pieces)
    ]
    for load in loads:
        load.start()
    for load, store in zip(loads, stores):
        load.wait()
        store.start()
    for store in stores:
        store.wait()


def local(n_blk, n_split, user_factors, item_factors, obs_items, obs_conf):
    u_dev, rank = user_factors.shape
    slab_rows = item_factors.shape[0]
    share_rows = slab_rows // n_split
    subs = obs_items.shape[1]
    items, confs = (obs.transpose(1, 2, 0) for obs in (obs_items, obs_conf))
    everyone = n_split * u_dev
    f32, b16 = jnp.float32, jnp.bfloat16
    dma = pltpu.SemaphoreType.DMA
    results = pl.pallas_call(
        functools.partial(kernel, n_blk, n_split),
        out_shape=(
            jax.ShapeDtypeStruct((u_dev, rank), f32),
            jax.ShapeDtypeStruct((share_rows, rank), f32),
        ),
        in_specs=[pl.BlockSpec(memory_space=pltpu.HBM)] * 4,
        out_specs=(pl.BlockSpec(memory_space=pl.ANY),) * 2,
        scratch_shapes=[
            pltpu.VMEM((everyone, rank), f32),
            pltpu.VMEM((everyone, rank), b16),
            pltpu.VMEM((everyone, rank), b16),
            pltpu.VMEM((3 * slab_rows, rank), b16),
            pltpu.VMEM((3 * slab_rows, everyone), b16),
            pltpu.VMEM((subs, slab_rows, everyone), f32),
            pltpu.VMEM((slab_rows, rank), f32),
            pltpu.VMEM((n_split,) + items.shape, jnp.int32),
            pltpu.VMEM((n_split,) + items.shape, jnp.int32),
            pltpu.VMEM((subs, COLS, slab_rows, rank // COLS), f32),
            pltpu.VMEM((subs - 1, COLS, slab_rows, rank // COLS), f32),
            pltpu.VMEM((COLS, share_rows, rank // COLS), f32),
            dma((3 + COLS,)),
            pltpu.SemaphoreType.REGULAR,
            dma((n_split - 1, 2, 2)),
            dma((n_split - 1, 2, 2)),
            dma((n_split - 1, PIECES)),
            dma((n_split - 1, PIECES)),
            dma((subs - 1, COLS)),
            dma((subs - 1, COLS)),
            dma((COLS,)),
            dma((COLS,)),
        ],
        compiler_params=pltpu.CompilerParams(
            collective_id=0, has_side_effects=True, vmem_limit_bytes=63 * 2**20
        ),
    )(user_factors, item_factors, items, confs)
    return pl.pallas_call(
        store_kernel,
        out_shape=tuple(jax.ShapeDtypeStruct(x.shape, x.dtype) for x in results),
        in_specs=[pl.BlockSpec(memory_space=pl.ANY)] * 2,
        out_specs=(pl.BlockSpec(memory_space=pl.ANY),) * 2,
        scratch_shapes=[
            *(pltpu.VMEM(x.shape, x.dtype) for x in results),
            dma((PARTS + 1,)),
            dma((PARTS + 1,)),
        ],
        compiler_params=pltpu.CompilerParams(vmem_limit_bytes=63 * 2**20),
    )(*results)


def solution(mesh):
    in_specs = (
        P(("blk", "split"), None),
        P("blk", None),
        P(("blk", "split"), None, None),
        P(("blk", "split"), None, None),
    )
    out_specs = (P(("blk", "split"), None), P(("blk", "split"), None))
    body = functools.partial(local, mesh.shape["blk"], mesh.shape["split"])
    return jax.shard_map(body, mesh=mesh, in_specs=in_specs, out_specs=out_specs, check_vma=False)
```

```python
import functools

import jax
import jax.numpy as jnp
from jax import lax
from jax.experimental import pallas as pl
from jax.experimental.pallas import tpu as pltpu
from jax.sharding import PartitionSpec as P

SUBS = 4


LEARN_RATE = 0.0005
CONF_SCALE = 0.5
RIDGE_COEF = 0.01

MESH = pl.DeviceIdType.MESH
PIECES = 4
PARTS = 2
COLS = 2


def halves(x):
    high = x.astype(jnp.bfloat16)
    return high, (x - high.astype(jnp.float32)).astype(jnp.bfloat16)


def dot(a, b, dims):
    return lax.dot_general(a, b, (dims, ((), ())), preferred_element_type=jnp.float32)


def stacked(a, b, dims):
    rows = a.shape[0] // 2
    both = dot(a, b[0], dims)
    return both[:rows] + (both[rows:] + dot(a[:rows], b[1], dims))


BOTH_LAST = ((1,), (1,))
PLAIN = ((1,), (0,))
BOTH_FIRST = ((0,), (0,))


def kernel(
    n_blk, n_split,
    u_hbm, h_hbm, item_hbm, conf_hbm, u_out, i_out,
    users, users_hi, users_lo, slab_16, err_16, counts, grad, item_in, conf_in,
    held, outgoing, share_buf,
    load_sem, turn_sem, obs_send, obs_recv, u_send, u_recv, h_send, h_recv, share_send, share_recv,
):
    u_dev, rank = u_hbm.shape
    slab_rows = h_hbm.shape[0]
    share_rows = slab_rows // n_split
    piece = u_dev // PIECES
    col = rank // COLS
    blk = lax.axis_index("blk")
    spl = lax.axis_index("split")
    ahead = lax.rem(blk + n_blk - 1, n_blk)
    behind = lax.rem(blk + 1, n_blk)
    peers = [lax.rem(spl + q, n_split) for q in range(n_split)]
    share_at = pl.multiple_of(spl * share_rows, share_rows)

    barrier = pltpu.get_barrier_semaphore()
    for q in range(1, n_split):
        pl.semaphore_signal(barrier, inc=1, device_id=(blk, peers[q]), device_id_type=MESH)
    for other in (ahead, behind):
        pl.semaphore_signal(barrier, inc=1, device_id=(other, spl), device_id_type=MESH)
    loads = [
        pltpu.make_async_copy(there, here, load_sem.at[i])
        for i, (there, here) in enumerate((
            (u_hbm, users.at[pl.ds(0, u_dev)]),
            (item_hbm, item_in.at[0]),
            (conf_hbm, conf_in.at[0]),
            *((h_hbm.at[:, pl.ds(c * col, col)], held.at[0, c]) for c in range(COLS)),
        ))
    ]
    for load in loads:
        load.start()
    pl.semaphore_wait(barrier, n_split + 1)

    def obs_copies(q, part, steps):
        slot = n_split - q
        copies = []
        for i, (here, there) in enumerate(((item_hbm, item_in), (conf_hbm, conf_in))):
            copy = pltpu.make_async_remote_copy(
                src_ref=here.at[steps], dst_ref=there.at[slot, steps],
                send_sem=obs_send.at[q - 1, part, i], recv_sem=obs_recv.at[slot - 1, part, i],
                device_id=(blk, peers[q]), device_id_type=MESH,
            )
            copies.append(copy)
        return copies

    first, rest = pl.ds(0, 2), pl.ds(2, SUBS - 2)
    first_obs = [None] + [obs_copies(q, 0, first) for q in range(1, n_split)]
    rest_obs = [None] + [obs_copies(q, 1, rest) for q in range(1, n_split)]
    for copies in first_obs[1:]:
        for copy in copies:
            copy.start()
    user_copies = [None] + [
        [
            pltpu.make_async_remote_copy(
                src_ref=u_hbm.at[pl.ds(p * piece, piece)],
                dst_ref=users.at[pl.ds((n_split - q) * u_dev + p * piece, piece)],
                send_sem=u_send.at[q - 1, p], recv_sem=u_recv.at[n_split - q - 1, p],
                device_id=(blk, peers[q]), device_id_type=MESH,
            )
            for p in range(PIECES)
        ]
        for q in range(1, n_split)
    ]

    def send_users():
        for q in range(1, n_split):
            for copy in user_copies[q]:
                copy.start()

    paired = n_blk % 2 == 0
    even = lax.rem(blk, 2) == 0 if paired else blk >= 0
    pl.when(even)(send_users)

    def count(q, start, stop):
        rows = lax.broadcasted_iota(jnp.int32, (slab_rows, u_dev), 0)

        @pl.loop(start, stop)
        def _(step):
            total = jnp.zeros((slab_rows, u_dev), jnp.float32)
            for k in range(item_in.shape[2]):
                item = item_in[q, step, k:k + 1, :]
                conf = conf_in[q, step, k:k + 1, :].astype(jnp.float32)
                total = total + jnp.where(rows == item, conf, 0.0)
            counts[step, :, q * u_dev:(q + 1) * u_dev] = total

    def errors(scores, r):
        target = jnp.where(r > 0, 1.0, 0.0).astype(jnp.float32)
        return (1.0 + CONF_SCALE * r) * (scores - target)

    def split_users(rows):
        high, low = halves(users[rows, :])
        users_hi[rows, :] = high
        users_lo[rows, :] = low

    def split_slab(step, c):
        columns = columns_of[c]
        high, low = halves(held[step, c])
        slab_16[0:slab_rows, columns] = high
        slab_16[slab_rows:2 * slab_rows, columns] = low
        slab_16[2 * slab_rows:, columns] = high

    def scores_of(rows, columns):
        return stacked(
            slab_16[0:2 * slab_rows, columns],
            (users_hi[rows, columns], users_lo[rows, columns]),
            BOTH_LAST,
        )

    def keep_errors(step, rows, scores):
        high, low = halves(errors(scores, counts[step, :, rows]))
        err_16[0:slab_rows, rows] = high
        err_16[slab_rows:2 * slab_rows, rows] = high
        err_16[2 * slab_rows:, rows] = low

    def item_grad(rows, columns):
        return stacked(
            err_16[slab_rows:, rows], (users_hi[rows, columns], users_lo[rows, columns]), PLAIN
        )

    def user_step(rows):
        grad_user = dot(err_16[:, rows], slab_16[...], BOTH_FIRST)
        old = users[rows, :]
        return old - LEARN_RATE * (grad_user + RIDGE_COEF * old)

    def slab_copy(step, c):
        return pltpu.make_async_remote_copy(
            src_ref=outgoing.at[step, c], dst_ref=held.at[step + 1, c],
            send_sem=h_send.at[step, c], recv_sem=h_recv.at[step, c],
            device_id=(ahead, spl), device_id_type=MESH,
        )

    def send_slab(step, c, total):
        old = held[step, c]
        outgoing[step, c] = old - LEARN_RATE * (total + RIDGE_COEF * old)
        slab_copy(step, c).start()

    whole = slice(0, rank)
    every = slice(0, n_split * u_dev)
    own = slice(0, u_dev)
    columns_of = [slice(c * col, (c + 1) * col) for c in range(COLS)]

    for load in loads:
        load.wait()
    split_users(own)
    for c in range(COLS):
        split_slab(0, c)
    count(0, 0, SUBS)
    keep_errors(0, own, scores_of(own, whole))
    grad[...] = item_grad(own, whole)
    for q in range(1, n_split):
        for copy in first_obs[n_split - q]:
            copy.wait_recv()
        count(q, 0, 2)
    if paired:

        @pl.when(jnp.logical_not(even))
        def _():
            pl.semaphore_wait(turn_sem, 1)
            send_users()

    part = u_dev // PARTS
    for q in range(1, n_split):
        for p in range(PIECES):
            user_copies[n_split - q][p].wait_recv()
            if paired and q == n_split - 1 and p == 0:

                @pl.when(even)
                def _():
                    pl.semaphore_signal(
                        turn_sem, inc=1, device_id=(behind, spl), device_id_type=MESH
                    )

            done = (p + 1) * piece
            if done % part == 0:
                rows = slice(q * u_dev + done - part, q * u_dev + done)
                split_users(rows)
                keep_errors(0, rows, scores_of(rows, whole))
                if q < n_split - 1 or p < PIECES - 1:
                    grad[...] += item_grad(rows, whole)
    for c, columns in enumerate(columns_of):
        send_slab(0, c, grad[:, columns] + item_grad(rows, columns))

    def update_users():
        @pl.loop(0, n_split)
        def _(q):
            rows = pl.ds(pl.multiple_of(q * u_dev, u_dev), u_dev)
            users[rows, :] = user_step(rows)
            split_users(rows)

    update_users()

    @pl.loop(1, SUBS - 1)
    def _(step):
        scores = 0.0
        for c, columns in enumerate(columns_of):
            slab_copy(step - 1, c).wait_recv()
            split_slab(step, c)
            scores = scores + scores_of(every, columns)
        keep_errors(step, every, scores)

        @pl.when(step == 1)
        def _():
            for copies in rest_obs[1:]:
                for copy in copies:
                    copy.start()

        for c, columns in enumerate(columns_of):
            send_slab(step, c, item_grad(every, columns))
        update_users()

        @pl.when(step == 1)
        def _():
            for q in range(1, n_split):
                for copy in rest_obs[n_split - q]:
                    copy.wait_recv()
                count(q, 2, SUBS)

    last = SUBS - 1
    share = pl.ds(share_at, share_rows)
    low_share = pl.ds(pl.multiple_of(slab_rows + share_at, share_rows), share_rows)
    scores = 0.0
    for c, columns in enumerate(columns_of):
        slab_copy(last - 1, c).wait_recv()
        split_slab(last, c)
        scores = scores + stacked(
            jnp.concatenate([slab_16[share, columns], slab_16[low_share, columns]], axis=0),
            (users_hi[:, columns], users_lo[:, columns]),
            BOTH_LAST,
        )
    share_errors = jnp.concatenate(halves(errors(scores, counts[last, share, :])), axis=0)
    share_copies = []
    for c, columns in enumerate(columns_of):
        total = stacked(share_errors, (users_hi[:, columns], users_lo[:, columns]), PLAIN)
        old = held[last, c, share, :]
        share_buf[c] = old - LEARN_RATE * (total + RIDGE_COEF * old)
        copy = pltpu.make_async_remote_copy(
            src_ref=share_buf.at[c], dst_ref=i_out.at[:, pl.ds(c * col, col)],
            send_sem=share_send.at[c], recv_sem=share_recv.at[c],
            device_id=(ahead, spl), device_id_type=MESH,
        )
        copy.start()
        share_copies.append(copy)
    keep_errors(last, own, scores_of(own, whole))
    users[own, :] = user_step(own)
    store = pltpu.make_async_copy(users.at[pl.ds(0, u_dev)], u_out, load_sem.at[0])
    store.start()

    for q in range(1, n_split):
        for copy in first_obs[q] + rest_obs[q] + user_copies[q]:
            copy.wait_send()
    for step in range(last):
        for c in range(COLS):
            slab_copy(step, c).wait_send()
    for copy in share_copies:
        copy.wait_send()
        copy.wait_recv()
    store.wait()


def store_kernel(u_in, i_in, u_out, i_out, u_buf, i_buf, load_sem, store_sem):
    rows = u_in.shape[0] // PARTS
    pieces = [(i_in, i_buf, i_out)]
    for p in range(PARTS):
        at = pl.ds(p * rows, rows)
        pieces.append((u_in.at[at], u_buf.at[at], u_out.at[at]))
    loads = [
        pltpu.make_async_copy(there, here, load_sem.at[i]) for i, (there, here, _) in enumerate(pieces)
    ]
    stores = [
        pltpu.make_async_copy(here, out, store_sem.at[i]) for i, (_, here, out) in enumerate(pieces)
    ]
    for load in loads:
        load.start()
    for load, store in zip(loads, stores):
        load.wait()
        store.start()
    for store in stores:
        store.wait()


def local(n_blk, n_split, user_factors, item_factors, obs_items, obs_conf):
    u_dev, rank = user_factors.shape
    slab_rows = item_factors.shape[0]
    share_rows = slab_rows // n_split
    subs = obs_items.shape[1]
    items, confs = (obs.transpose(1, 2, 0) for obs in (obs_items, obs_conf))
    everyone = n_split * u_dev
    f32, b16 = jnp.float32, jnp.bfloat16
    dma = pltpu.SemaphoreType.DMA
    results = pl.pallas_call(
        functools.partial(kernel, n_blk, n_split),
        out_shape=(
            jax.ShapeDtypeStruct((u_dev, rank), f32),
            jax.ShapeDtypeStruct((share_rows, rank), f32),
        ),
        in_specs=[pl.BlockSpec(memory_space=pltpu.HBM)] * 4,
        out_specs=(pl.BlockSpec(memory_space=pl.ANY),) * 2,
        scratch_shapes=[
            pltpu.VMEM((everyone, rank), f32),
            pltpu.VMEM((everyone, rank), b16),
            pltpu.VMEM((everyone, rank), b16),
            pltpu.VMEM((3 * slab_rows, rank), b16),
            pltpu.VMEM((3 * slab_rows, everyone), b16),
            pltpu.VMEM((subs, slab_rows, everyone), f32),
            pltpu.VMEM((slab_rows, rank), f32),
            pltpu.VMEM((n_split,) + items.shape, jnp.int32),
            pltpu.VMEM((n_split,) + items.shape, jnp.int32),
            pltpu.VMEM((subs, COLS, slab_rows, rank // COLS), f32),
            pltpu.VMEM((subs - 1, COLS, slab_rows, rank // COLS), f32),
            pltpu.VMEM((COLS, share_rows, rank // COLS), f32),
            dma((3 + COLS,)),
            pltpu.SemaphoreType.REGULAR,
            dma((n_split - 1, 2, 2)),
            dma((n_split - 1, 2, 2)),
            dma((n_split - 1, PIECES)),
            dma((n_split - 1, PIECES)),
            dma((subs - 1, COLS)),
            dma((subs - 1, COLS)),
            dma((COLS,)),
            dma((COLS,)),
        ],
        compiler_params=pltpu.CompilerParams(
            collective_id=0, has_side_effects=True, vmem_limit_bytes=63 * 2**20
        ),
    )(user_factors, item_factors, items, confs)
    return pl.pallas_call(
        store_kernel,
        out_shape=tuple(jax.ShapeDtypeStruct(x.shape, x.dtype) for x in results),
        in_specs=[pl.BlockSpec(memory_space=pl.ANY)] * 2,
        out_specs=(pl.BlockSpec(memory_space=pl.ANY),) * 2,
        scratch_shapes=[
            *(pltpu.VMEM(x.shape, x.dtype) for x in results),
            dma((PARTS + 1,)),
            dma((PARTS + 1,)),
        ],
        compiler_params=pltpu.CompilerParams(vmem_limit_bytes=63 * 2**20),
    )(*results)


def solution(mesh):
    in_specs = (
        P(("blk", "split"), None),
        P("blk", None),
        P(("blk", "split"), None, None),
        P(("blk", "split"), None, None),
    )
    out_specs = (P(("blk", "split"), None), P(("blk", "split"), None))
    body = functools.partial(local, mesh.shape["blk"], mesh.shape["split"])
    return jax.shard_map(body, mesh=mesh, in_specs=in_specs, out_specs=out_specs, check_vma=False)
```
